256 devices in a mesh: sample: 16 (over z, core), feature: 16 (over y, x).
Axes of the slice: x: 4, y: 4, z: 8, core: 2. Of those that a mesh axis runs over, the one named last changes fastest.
Arguments:
- slab: bfloat16 [49152, 16384], P('sample', 'feature'), may hold values from -20 to 20
- omega: int32 [16384, 512], P('feature'), may hold values from -8 to 8
Outputs:
- coeffs: float32 [512, 16384], P('sample', 'feature')
- factor: float32 [512, 512], replicated
The draws below stay inside these ranges and needn't reach their ends.
All inputs are finite; a program needn't handle non-finite values.
Results may differ from the reference program's by a relative error of at most 0.0019.
Values may be sent and summed in bfloat16 or wider, within the bound.
A program may use at most 128 MiB of HBM per device.

```python
import math
import jax
import jax.numpy as jnp
from jax import lax

D = 16384
K = 512
TOKENS = 49152


def draw_slab(key, part):
    key = jax.random.fold_in(key, 11)
    key_noise, key_rows, key_cols = jax.random.split(key, 3)
    row_scale = jnp.exp(jax.random.uniform(key_rows, (TOKENS, 1), jnp.float32, math.log(0.3), math.log(3.0)))
    col_scale = jnp.exp(jax.random.uniform(key_cols, (1, D), jnp.float32, math.log(0.3), math.log(3.0)))
    noise = jax.random.truncated_normal(key_noise, -4.0, 4.0, (TOKENS, D), jnp.float32)
    return (noise * row_scale * col_scale / 2.0).astype(jnp.bfloat16)


def set_ends(values, own_key, low, high):
    spot = [jax.random.randint(jax.random.fold_in(own_key, axis), (), 0, length) for axis, length in enumerate(values.shape)]
    widest = values.shape.index(max(values.shape))
    beside = spot[:widest] + [(spot[widest] + 1) % values.shape[widest]] + spot[widest + 1:]
    return values.at[tuple(spot)].set(low).at[tuple(beside)].set(high)


def setup_inputs(seed: int = 0) -> dict:
    splits = jax.random.split(jax.random.key(seed), 3)
    slab = draw_slab(jax.random.fold_in(splits[2], 71), 0)
    omega = set_ends(jax.random.randint(splits[1], (D, K), -8, 9), jax.random.fold_in(splits[1], 1), -8, 8).astype(jnp.int32)
    return dict(slab=slab, omega=omega)


def reference(slab, omega):
    omega_b = omega.astype(jnp.bfloat16)
    scale = 1.0 / math.sqrt(24.0 * D)
    sketch = jnp.dot(slab.astype(jnp.float32), omega_b.astype(jnp.float32), preferred_element_type=jnp.float32) * scale
    gram = jnp.dot(sketch.T.astype(jnp.float32), sketch.astype(jnp.float32), preferred_element_type=jnp.float32, precision=lax.Precision.HIGHEST)
    lower = jnp.linalg.cholesky(gram)
    basis_t = lax.linalg.triangular_solve(lower, sketch.T, left_side=True, lower=True).astype(jnp.bfloat16)
    coeffs = jnp.dot(basis_t.astype(jnp.float32), slab.astype(jnp.float32), preferred_element_type=jnp.float32)
    factor = lower.T / math.sqrt(TOKENS)
    return (coeffs, factor)
```

```python
import functools
import math

import jax
import jax.numpy as jnp
from jax import lax
from jax.experimental import pallas as pl
from jax.experimental.pallas import tpu as pltpu
from jax.sharding import PartitionSpec as P

D = 16384
F32 = jnp.float32
BF16 = jnp.bfloat16
HIGH = lax.Precision.HIGHEST
MIB = 1 << 20
B = 128
VMEM = pl.BlockSpec(memory_space=pltpu.VMEM)


def remote(src, dst, send_sem, recv_sem, axis, index):
    return pltpu.make_async_remote_copy(
        src_ref=src,
        dst_ref=dst,
        send_sem=send_sem,
        recv_sem=recv_sem,
        device_id={axis: index},
        device_id_type=pl.DeviceIdType.MESH,
    )


def greet(barrier, axis, index):
    pl.semaphore_signal(barrier, inc=1, device_id={axis: index}, device_id_type=pl.DeviceIdType.MESH)


def sketch_kernel(scale, slab_ref, omega_ref, y_ref, wide, tx1, rx1, side1, own1, tx2, rx2, sum2, send_sem, recv_sem):
    f = lax.axis_index("feature")
    x, y = lax.rem(f, 4), f // 4

    def node(axis, pos):
        return 4 * y + pos if axis == 0 else 4 * pos + x

    here = (x, y)
    barrier = pltpu.get_barrier_semaphore()
    for axis in range(2):
        for step in (1, 3):
            greet(barrier, "feature", node(axis, lax.rem(here[axis] + step, 4)))

    wide[...] = omega_ref[...].astype(BF16)
    part = y_ref.shape[1]
    big = 4 * part
    cut = big // 2
    small = part // 2

    def rows(half, pos):
        start = half * 16 * part
        if half == 0:
            blocks = [start + (4 * j + pos) * part for j in range(4)]
            return jnp.concatenate([slab_ref[pl.ds(pl.multiple_of(b, 16), part), :] for b in blocks], axis=0)
        return slab_ref[pl.ds(pl.multiple_of(start + pos * big, 16), big), :]

    def product(half, pos):
        return jnp.dot(rows(half, pos), wide[...], preferred_element_type=F32)

    def send(stage, half, way, piece):
        axis = half if stage == 0 else 1 - half
        to = node(axis, lax.rem(here[axis] + (1 if way == 0 else 3), 4))
        at = ((stage * 2 + half) * 2 + way) * 3 + piece
        tx, rx = (tx1, rx1) if stage == 0 else (tx2, rx2)
        return remote(
            tx.at[half, way, piece], rx.at[half, way, piece], send_sem.at[at], recv_sem.at[at], "feature", to
        )

    copies = []

    def go(*which):
        copy = send(*which)
        copy.start()
        copies.append(copy)

    first = True
    for half in range(2):
        pos = here[half]
        far = product(half, lax.rem(pos + 2, 4)).astype(BF16)
        tx1[half, 0, 0] = far[:cut]
        tx1[half, 1, 0] = far[cut:]
        if first:
            pl.semaphore_wait(barrier, 4)
            first = False
        go(0, half, 0, 0)
        go(0, half, 1, 0)
    for half in range(2):
        pos = here[half]
        right = product(half, lax.rem(pos + 1, 4))
        tx1[half, 0, 1] = right[cut:].astype(BF16)
        go(0, half, 0, 1)
        side1[half, 0] = right[:cut]
        left = product(half, lax.rem(pos + 3, 4))
        tx1[half, 1, 1] = left[:cut].astype(BF16)
        go(0, half, 1, 1)
        side1[half, 1] = left[cut:]
    for half in range(2):
        for way in range(2):
            send(0, half, way, 0).wait_recv()
            tx1[half, way, 2] = (side1[half, way] + rx1[half, way, 0].astype(F32)).astype(BF16)
            go(0, half, way, 2)
    for half in range(2):
        own1[half] = product(half, here[half])
    for half in range(2):
        for way in range(2):
            send(0, half, way, 1).wait_recv()
        own1[half, cut:] += rx1[half, 0, 1].astype(F32)
        own1[half, :cut] += rx1[half, 1, 1].astype(F32)
        for way in range(2):
            send(0, half, way, 2).wait_recv()
        own1[half, :cut] += rx1[half, 0, 2].astype(F32)
        own1[half, cut:] += rx1[half, 1, 2].astype(F32)

        def block(pos, lo, hi):
            return own1[half, pl.ds(pl.multiple_of(pos * part + lo, 8), hi - lo), :]

        pos = here[1 - half]
        far, right, left = (lax.rem(pos + step, 4) for step in (2, 1, 3))
        tx2[half, 0, 0] = block(far, 0, small)
        go(1, half, 0, 0)
        tx2[half, 1, 0] = block(far, small, part)
        go(1, half, 1, 0)
        tx2[half, 0, 1] = block(right, small, part)
        go(1, half, 0, 1)
        tx2[half, 1, 1] = block(left, 0, small)
        go(1, half, 1, 1)
        tx2[half, 0, 2] = block(right, 0, small)
        tx2[half, 1, 2] = block(left, small, part)
        sum2[half] = block(pos, 0, part)
    for half in range(2):
        for way in range(2):
            send(1, half, way, 0).wait_recv()
            tx2[half, way, 2] += rx2[half, way, 0]
            go(1, half, way, 2)
    for half in range(2):
        for way in range(2):
            send(1, half, way, 1).wait_recv()
            send(1, half, way, 2).wait_recv()
        y_ref[half, small:] = (sum2[half, small:] + (rx2[half, 0, 1] + rx2[half, 1, 2])) * scale
        y_ref[half, :small] = (sum2[half, :small] + (rx2[half, 1, 1] + rx2[half, 0, 2])) * scale
    for copy in copies:
        copy.wait_send()


def sketch_part(slab, omega):
    tokens, depth = slab.shape
    k = omega.shape[1]
    part = tokens // 32
    big, cut, small = 4 * part, 2 * part, part // 2
    return pl.pallas_call(
        functools.partial(sketch_kernel, 1.0 / math.sqrt(24.0 * D)),
        out_shape=jax.ShapeDtypeStruct((2, part, k), F32),
        in_specs=[VMEM, VMEM],
        out_specs=VMEM,
        scratch_shapes=[
            pltpu.VMEM((depth, k), BF16),
            pltpu.VMEM((2, 2, 3, cut, k), BF16),
            pltpu.VMEM((2, 2, 3, cut, k), BF16),
            pltpu.VMEM((2, 2, cut, k), F32),
            pltpu.VMEM((2, big, k), F32),
            pltpu.VMEM((2, 2, 3, small, k), F32),
            pltpu.VMEM((2, 2, 3, small, k), F32),
            pltpu.VMEM((2, part, k), F32),
            pltpu.SemaphoreType.DMA((24,)),
            pltpu.SemaphoreType.DMA((24,)),
        ],
        compiler_params=pltpu.CompilerParams(collective_id=0, has_side_effects=True, vmem_limit_bytes=48 * MIB),
        name="sketch",
    )(slab, omega)


def gram_kernel(y_ref, out_ref, packed, rx0, half, rx1, rx2, send_sem, recv_sem):
    f, s = lax.axis_index("feature"), lax.axis_index("sample")
    z, c = s // 2, lax.rem(s, 2)
    twin = 2 * z + 1 - c
    nf = lax.axis_size("feature")
    nz = lax.axis_size("sample") // 2
    barrier = pltpu.get_barrier_semaphore()
    greet(barrier, "sample", twin)
    for d in range(1, nf):
        greet(barrier, "feature", lax.rem(f + d, nf))
    for d in range(1, nz):
        greet(barrier, "sample", lax.rem(s + 2 * d, 2 * nz))

    k = y_ref.shape[2]
    y = y_ref[...].reshape(-1, k)
    yt = y.T
    nb = k // B
    at = 0
    for i in range(nb):
        row = jnp.dot(yt[i * B : (i + 1) * B], y[:, : (i + 1) * B], precision=HIGH, preferred_element_type=F32)
        for j in range(i + 1):
            packed[at * B : (at + 1) * B, :] = row[:, j * B : (j + 1) * B]
            at += 1
    mine = at * B // 2
    part = mine // nf
    pl.semaphore_wait(barrier, nf + nz - 1)

    copies = []

    def go(n, src, dst, axis, index):
        copy = remote(src, dst, send_sem.at[n], recv_sem.at[n], axis, index)
        copy.start()
        copies.append(copy)
        return copy

    base = pl.multiple_of(c * mine, 8)
    other = pl.multiple_of((1 - c) * mine, 8)
    go(0, packed.at[pl.ds(other, mine)], rx0, "sample", twin).wait_recv()
    half[...] = packed[pl.ds(base, mine), :] + rx0[...]

    def share(p):
        return pl.ds(pl.multiple_of(p * part, 8), part)

    got = []
    for d in range(1, nf):
        to = lax.rem(f + d, nf)
        got.append(go(d, half.at[share(to)], rx1.at[d - 1], "feature", to))
    for copy in got:
        copy.wait_recv()
    total = half[share(f), :]
    for d in range(1, nf):
        total += rx1[d - 1]
    rx2[z] = total
    got = []
    for d in range(1, nz):
        to = lax.rem(s + 2 * d, 2 * nz)
        got.append(go(nf + d, rx2.at[z], rx2.at[z], "sample", to))
    for copy in got:
        copy.wait_recv()
    total = rx2[0]
    for d in range(1, nz):
        total += rx2[d]
    own = pl.ds(pl.multiple_of(c * mine + f * part, 8), part)
    out_ref[own, :] = total
    got = []
    for d in range(1, nf):
        got.append(go(nf + nz + d, out_ref.at[own], out_ref.at[own], "feature", lax.rem(f + d, nf)))
    for copy in got:
        copy.wait_recv()
    whole = pl.ds(base, mine)
    go(2 * nf + nz, out_ref.at[whole], out_ref.at[whole], "sample", twin).wait_recv()
    for copy in copies:
        copy.wait_send()


def gram_all(y):
    k = y.shape[2]
    nb = k // B
    rows = nb * (nb + 1) // 2 * B
    nf, nz = lax.axis_size("feature"), lax.axis_size("sample") // 2
    mine = rows // 2
    part = mine // nf
    return pl.pallas_call(
        gram_kernel,
        out_shape=jax.ShapeDtypeStruct((rows, B), F32),
        in_specs=[VMEM],
        out_specs=VMEM,
        scratch_shapes=[
            pltpu.VMEM((rows, B), F32),
            pltpu.VMEM((mine, B), F32),
            pltpu.VMEM((mine, B), F32),
            pltpu.VMEM((nf - 1, part, B), F32),
            pltpu.VMEM((nz, part, B), F32),
            pltpu.SemaphoreType.DMA((2 * nf + nz + 1,)),
            pltpu.SemaphoreType.DMA((2 * nf + nz + 1,)),
        ],
        compiler_params=pltpu.CompilerParams(collective_id=1, has_side_effects=True, vmem_limit_bytes=32 * MIB),
        name="gram",
    )(y)


def rep(x, shape=(8, 128)):
    return jnp.broadcast_to(x, shape)

def chol_block(s, x):
    n = len(s)
    s, x = list(s), list(x)
    ux = []
    for p in range(n):
        k = {}
        for q in range(p + 1, min(n, p + 2)):
            for c in range(8):
                k[q, c] = rep(s[q][:, 8 * p + c : 8 * p + c + 1])
        rg = [rep(s[p][r : r + 1, :]) for r in range(8)]
        rx = [rep(x[p][r : r + 1, :]) for r in range(8)]
        e = {}
        for c in range(8):
            col = rep(s[p][:, 8 * p + c : 8 * p + c + 1])
            for r in range(c, 8):
                e[r, c] = rep(col[r : r + 1, :])
        m = {}
        inv = []
        for r in range(8):
            inv.append(1.0 / e[r, r])
            for t in range(r + 1, 8):
                m[t, r] = e[t, r] * inv[r]
            for t in range(r + 1, 8):
                for c in range(r + 1, t + 1):
                    e[t, c] = e[t, c] - m[t, r] * e[c, r]
            for t in range(r + 1, 8):
                rg[t] = rg[t] - m[t, r] * rg[r]
                rx[t] = rx[t] - m[t, r] * rx[r]
        root = [lax.rsqrt(e[r, r]) for r in range(8)]
        sub = lax.broadcasted_iota(jnp.int32, (8, 128), 0)
        ox = rx[0] * root[0]
        for r in range(1, 8):
            ox = jnp.where(sub == r, rx[r] * root[r], ox)
        ux.append(ox)
        if p + 1 < n:
            wg = [rg[r] * inv[r] for r in range(8)]
            wx = [rx[r] * inv[r] for r in range(8)]
            for r in range(7, -1, -1):
                for t in range(r):
                    wg[t] = wg[t] - m[r, t] * wg[r]
                    wx[t] = wx[t] - m[r, t] * wx[r]
            for q in range(p + 1, n):
                if q > p + 1:
                    for c in range(8):
                        k[q, c] = rep(s[q][:, 8 * p + c : 8 * p + c + 1])
                tg = [k[q, c] * wg[c] for c in range(8)]
                tx = [k[q, c] * wx[c] for c in range(8)]
                s[q] = s[q] - (((tg[0] + tg[1]) + (tg[2] + tg[3])) + ((tg[4] + tg[5]) + (tg[6] + tg[7])))
                x[q] = x[q] - (((tx[0] + tx[1]) + (tx[2] + tx[3])) + ((tx[4] + tx[5]) + (tx[6] + tx[7])))
    return ux

def factor_kernel(tokens, g_ref, lt_ref, inv_ref, w):
    n = w.shape[0]
    at = 0
    for i in range(n // B):
        for j in range(i + 1):
            tile = g_ref[at * B : (at + 1) * B, :]
            w[i * B : (i + 1) * B, j * B : (j + 1) * B] = tile
            if j < i:
                w[j * B : (j + 1) * B, i * B : (i + 1) * B] = tile.T
            at += 1
    scale = 1.0 / math.sqrt(tokens)
    inv_ref[...] = jnp.zeros_like(inv_ref)
    lt_ref[...] = jnp.zeros_like(lt_ref)

    def finish(k, low):
        at, end = k * B, (k + 1) * B
        here = slice(at, end)
        rows = lax.broadcasted_iota(jnp.int32, (B, B), 0)
        cols = lax.broadcasted_iota(jnp.int32, (B, B), 1)
        upper = jnp.dot(low, w[here, here], precision=HIGH, preferred_element_type=F32)
        lt_ref[here, here] = jnp.where(cols >= rows, upper, 0.0) * scale
        inv_ref[here, here] = low
        if at:
            left = jnp.dot(low, w[here, :at], precision=HIGH, preferred_element_type=F32)
            inv_ref[here, :at] = left
        if end < n:
            right = jnp.dot(low, w[here, end:], precision=HIGH, preferred_element_type=F32)
            lt_ref[here, end:] = right * scale
            coef = right.T
            def dot(z):
                return jnp.dot(coef, z, precision=HIGH, preferred_element_type=F32)
            w[end:, end:] -= dot(right)
            w[end:, here] = -dot(low)
            if at:
                w[end:, :at] -= dot(left)

    def step(k, _):
        at = pl.multiple_of(k * B, B)
        here = pl.ds(at, B)
        rid = lax.broadcasted_iota(jnp.int32, (8, B), 0)
        cid = lax.broadcasted_iota(jnp.int32, (8, B), 1)
        s = [w[pl.ds(at + 8 * q, 8), here] for q in range(B // 8)]
        x = [jnp.where(rid + 8 * q == cid, 1.0, 0.0) for q in range(B // 8)]
        ux = chol_block(s, x)
        low = jnp.concatenate(ux, axis=0)
        for j in range(n // B):
            pl.when(k == j)(functools.partial(finish, j, low))
        return 0

    lax.fori_loop(0, n // B, step, 0)


def factor_all(gram, k, tokens):
    return pl.pallas_call(
        functools.partial(factor_kernel, tokens),
        out_shape=(jax.ShapeDtypeStruct((k, k), F32),) * 2,
        in_specs=[VMEM],
        out_specs=[VMEM, VMEM],
        scratch_shapes=[pltpu.VMEM((k, k), F32)],
        compiler_params=pltpu.CompilerParams(vmem_limit_bytes=32 * MIB),
        cost_estimate=pl.CostEstimate(flops=10**10, bytes_accessed=4 * MIB, transcendentals=0),
        name="factor",
    )(gram)


def split(a):
    hi = a.astype(BF16)
    return hi, (a - hi.astype(F32)).astype(BF16)


def project_kernel(inv_ref, z_ref, out_ref, tx0, rx0, own, tx, rx, send_sem, recv_sem):
    s = lax.axis_index("sample")
    nz = lax.axis_size("sample") // 2
    z, c = s // 2, lax.rem(s, 2)
    twin = 2 * z + 1 - c
    ways = [2 * lax.rem(z + 1, nz) + c, 2 * lax.rem(z + nz - 1, nz) + c]
    barrier = pltpu.get_barrier_semaphore()
    for to in (twin, *ways):
        greet(barrier, "sample", to)
    part = out_ref.shape[0]
    cols = out_ref.shape[1] // 2
    cut = part // 2
    hops = nz // 2

    def rows(core):
        picked = [inv_ref[pl.ds(pl.multiple_of((2 * j + core) * part, 8), part), :] for j in range(nz)]
        return split(jnp.concatenate(picked, axis=0))

    def dot(a, b):
        return jnp.dot(a, b, preferred_element_type=F32)

    theirs, ours = rows(1 - c), rows(c)
    copies = []

    def go(n, src, dst, to):
        copy = remote(src, dst, send_sem.at[n], recv_sem.at[n], "sample", to)
        copy.start()
        copies.append(copy)
        return copy

    pair = []
    for h in range(2):
        zh, zl = split(z_ref[:, h * cols : (h + 1) * cols])
        tx0[h] = dot(theirs[0], zh) + (dot(theirs[0], zl) + dot(theirs[1], zh))
        if h == 0:
            pl.semaphore_wait(barrier, 3)
        pair.append(go(h, tx0.at[h], rx0.at[h], twin))
        own[h] = dot(ours[0], zh) + (dot(ours[0], zl) + dot(ours[1], zh))

    def chunk(h, pos, lo=0, hi=part):
        return own[h, pl.ds(pl.multiple_of(pos * part + lo, 8), hi - lo), :]

    ring = {}

    def hop(h, way, j):
        n = 2 + (h * 2 + way) * hops + j
        rows_ = slice(0, cut) if j == 0 else slice(0, part)
        ring[h, way, j] = go(n, tx.at[h, way, j, rows_], rx.at[h, way, j, rows_], ways[way])

    for h in range(2):
        pair[h].wait_recv()
        own[h] += rx0[h]
        far = lax.rem(z + hops, nz)
        tx[h, 0, 0, :cut] = chunk(h, far, 0, cut)
        hop(h, 0, 0)
        tx[h, 1, 0, :cut] = chunk(h, far, cut, part)
        hop(h, 1, 0)
    for j in range(1, hops):
        for h in range(2):
            for way in range(2):
                pos = lax.rem(z + (hops - j if way == 0 else nz - hops + j), nz)
                ring[h, way, j - 1].wait_recv()
                if j == 1:
                    lo, hi = (0, cut) if way == 0 else (cut, part)
                    rest = (cut, part) if way == 0 else (0, cut)
                    tx[h, way, j, lo:hi] = chunk(h, pos, lo, hi) + rx[h, way, 0, :cut]
                    tx[h, way, j, rest[0] : rest[1]] = chunk(h, pos, *rest)
                else:
                    tx[h, way, j] = chunk(h, pos) + rx[h, way, j - 1]
                hop(h, way, j)
    for h in range(2):
        ring[h, 0, hops - 1].wait_recv()
        ring[h, 1, hops - 1].wait_recv()
        out_ref[:, h * cols : (h + 1) * cols] = chunk(h, z) + (rx[h, 0, hops - 1] + rx[h, 1, hops - 1])
    for copy in copies:
        copy.wait_send()


def project_all(inv, zp):
    k, width = zp.shape
    n = lax.axis_size("sample")
    part, cols, hops = k // n, width // 2, n // 4
    ring = (2, 2, hops, part, cols)
    return pl.pallas_call(
        project_kernel,
        out_shape=jax.ShapeDtypeStruct((part, width), F32),
        in_specs=[VMEM, VMEM],
        out_specs=VMEM,
        scratch_shapes=[
            pltpu.VMEM((2, k // 2, cols), F32),
            pltpu.VMEM((2, k // 2, cols), F32),
            pltpu.VMEM((2, k // 2, cols), F32),
            pltpu.VMEM(ring, F32),
            pltpu.VMEM(ring, F32),
            pltpu.SemaphoreType.DMA((2 + 4 * hops,)),
            pltpu.SemaphoreType.DMA((2 + 4 * hops,)),
        ],
        compiler_params=pltpu.CompilerParams(collective_id=2, has_side_effects=True, vmem_limit_bytes=32 * MIB),
        name="project",
    )(inv, zp)


def shards(slab, omega):
    tokens, width = slab.shape
    k = omega.shape[1]
    y = sketch_part(slab, omega)
    halves = [lax.all_gather(y[h].astype(BF16), "feature", axis=0, tiled=True) for h in range(2)]
    lt, inv = factor_all(gram_all(y), k, tokens * lax.axis_size("sample"))
    zp = sum(
        lax.dot_general(
            halves[h],
            slab[h * tokens // 2 : (h + 1) * tokens // 2],
            (((0,), (0,)), ((), ())),
            preferred_element_type=F32,
        )
        for h in range(2)
    )
    return project_all(inv, zp), lt


def solution(mesh):
    placed = (P("sample", "feature"), P("feature", None))
    return jax.shard_map(
        shards, mesh=mesh, in_specs=placed, out_specs=(P("sample", "feature"), P()), check_vma=False
    )
```

```python
import functools
import math

import jax
import jax.numpy as jnp
from jax import lax
from jax.experimental import pallas as pl
from jax.experimental.pallas import tpu as pltpu
from jax.sharding import PartitionSpec as P

D = 16384
F32 = jnp.float32
BF16 = jnp.bfloat16
HIGH = lax.Precision.HIGHEST
MIB = 1 << 20
B = 128
VMEM = pl.BlockSpec(memory_space=pltpu.VMEM)


def remote(src, dst, send_sem, recv_sem, axis, index):
    return pltpu.make_async_remote_copy(
        src_ref=src,
        dst_ref=dst,
        send_sem=send_sem,
        recv_sem=recv_sem,
        device_id={axis: index},
        device_id_type=pl.DeviceIdType.MESH,
    )


def greet(barrier, axis, index):
    pl.semaphore_signal(barrier, inc=1, device_id={axis: index}, device_id_type=pl.DeviceIdType.MESH)


def rep(a):
    return jnp.broadcast_to(a, a.shape[:-2] + (8, 128))


def inverse_factor(s, hook):
    n = s.shape[0]
    sub = lax.broadcasted_iota(jnp.int32, (8, 128), 0)
    lane = lax.broadcasted_iota(jnp.int32, (8, 128), 1)
    s = [s[q] for q in range(n)]
    x = [jnp.where(sub + 8 * q == lane, 1.0, 0.0) for q in range(n)]
    out = []
    for p in range(n):
        if p == n // 2:
            hook()
        cols = [rep(s[p][:, 8 * p + c : 8 * p + c + 1]) for c in range(8)]
        e = [jnp.stack([rep(cols[c][r : r + 1]) for r in range(c, 8)]) for c in range(8)]
        rg = jnp.stack([rep(s[p][r : r + 1]) for r in range(8)])
        rx = jnp.stack([rep(x[p][r : r + 1]) for r in range(8)])
        m, inv, wg, wx = [], [], [], []
        for r in range(8):
            inv.append(1.0 / e[r][0])
            root = lax.rsqrt(e[r][0])
            o = rx[0] * root
            ox = o if r == 0 else jnp.where(sub == r, o, ox)
            wg.append(rg[0] * inv[r])
            wx.append(rx[0] * inv[r])
            if r == 7:
                break
            m.append(e[r][1:] * inv[r])
            for c in range(r + 1, 8):
                e[c] = e[c] - m[r][c - r - 1 :] * e[r][c - r]
            rg = rg[1:] - m[r] * rg[0]
            rx = rx[1:] - m[r] * rx[0]
        out.append(ox)
        if p + 1 < n:
            for r in range(7, 0, -1):
                for t in range(r):
                    wg[t] = wg[t] - m[t][r - t - 1] * wg[r]
                    wx[t] = wx[t] - m[t][r - t - 1] * wx[r]
            for q in range(p + 1, n):
                k = [rep(s[q][:, 8 * p + c : 8 * p + c + 1]) for c in range(8)]
                for w, v in ((wg, s), (wx, x)):
                    t = [k[c] * w[c] for c in range(8)]
                    v[q] = v[q] - (((t[0] + t[1]) + (t[2] + t[3])) + ((t[4] + t[5]) + (t[6] + t[7])))
    return jnp.concatenate(out, axis=0)


def high(a, b):
    return jnp.dot(a, b, precision=HIGH, preferred_element_type=F32)


def kernel(
    scale, tokens, slab_ref, omega_ref, out_ref, factor_ref,
    wide, tx1, rx1, side1, own1, tx2, rx2, sum2,
    yall, packed, rx0, half_ref, rxp, rxz, gsum,
    zacc, rxt, txr, rxr, zc, cout, w, inv_ref, send_sem, recv_sem,
):
    f, s = lax.axis_index("feature"), lax.axis_index("sample")
    nf, nz = lax.axis_size("feature"), lax.axis_size("sample") // 2
    x, y = lax.rem(f, 4), f // 4
    z, c = s // 2, lax.rem(s, 2)
    twin = 2 * z + 1 - c
    barrier = pltpu.get_barrier_semaphore()
    greet(barrier, "sample", twin)
    for d in range(1, nf):
        greet(barrier, "feature", lax.rem(f + d, nf))
    for d in range(1, nz):
        greet(barrier, "sample", lax.rem(s + 2 * d, 2 * nz))

    copies = []
    count = [0]

    def plan(src, dst, axis, to):
        n = count[0]
        count[0] += 1
        copy = remote(src, dst, send_sem.at[n], recv_sem.at[n], axis, to)
        copies.append(copy)
        return copy

    def go(src, dst, axis, to):
        copy = plan(src, dst, axis, to)
        copy.start()
        return copy

    here = (x, y)

    def node(axis, pos):
        return 4 * y + pos if axis == 0 else 4 * pos + x

    def beside(axis, way):
        return node(axis, lax.rem(here[axis] + (1 if way == 0 else 3), 4))

    wide[...] = omega_ref[...].astype(BF16)
    part = yall.shape[3]
    k = yall.shape[4]
    big = 4 * part
    cut = big // 2
    small = part // 2

    def rows(half, pos):
        start = half * 16 * part
        if half == 0:
            blocks = [start + (4 * j + pos) * part for j in range(4)]
            return jnp.concatenate([slab_ref[pl.ds(pl.multiple_of(b, 16), part), :] for b in blocks], axis=0)
        return slab_ref[pl.ds(pl.multiple_of(start + pos * big, 16), big), :]

    def product(half, pos):
        return jnp.dot(rows(half, pos), wide[...], preferred_element_type=F32)

    sent = {}

    def pass_on(stage, half, way, piece):
        axis = half if stage == 0 else 1 - half
        tx, rx = (tx1, rx1) if stage == 0 else (tx2, rx2)
        sent[stage, half, way, piece] = go(
            tx.at[half, way, piece], rx.at[half, way, piece], "feature", beside(axis, way)
        )

    for half in range(2):
        pos = here[half]
        far = product(half, lax.rem(pos + 2, 4)).astype(BF16)
        tx1[half, 0, 0] = far[:cut]
        tx1[half, 1, 0] = far[cut:]
        if half == 0:
            pl.semaphore_wait(barrier, nf + nz - 1)
        pass_on(0, half, 0, 0)
        pass_on(0, half, 1, 0)
    for half in range(2):
        pos = here[half]
        right = product(half, lax.rem(pos + 1, 4))
        tx1[half, 0, 1] = right[cut:].astype(BF16)
        pass_on(0, half, 0, 1)
        side1[half, 0] = right[:cut]
        left = product(half, lax.rem(pos + 3, 4))
        tx1[half, 1, 1] = left[:cut].astype(BF16)
        pass_on(0, half, 1, 1)
        side1[half, 1] = left[cut:]
    for half in range(2):
        for way in range(2):
            sent[0, half, way, 0].wait_recv()
            tx1[half, way, 2] = (side1[half, way] + rx1[half, way, 0].astype(F32)).astype(BF16)
            pass_on(0, half, way, 2)
    for half in range(2):
        own1[half] = product(half, here[half])
    for half in range(2):
        for way in range(2):
            sent[0, half, way, 1].wait_recv()
        own1[half, cut:] += rx1[half, 0, 1].astype(F32)
        own1[half, :cut] += rx1[half, 1, 1].astype(F32)
        for way in range(2):
            sent[0, half, way, 2].wait_recv()
        own1[half, :cut] += rx1[half, 0, 2].astype(F32)
        own1[half, cut:] += rx1[half, 1, 2].astype(F32)

        def block(pos, lo, hi):
            return own1[half, pl.ds(pl.multiple_of(pos * part + lo, 8), hi - lo), :]

        pos = here[1 - half]
        far, right, left = (lax.rem(pos + step, 4) for step in (2, 1, 3))
        tx2[half, 0, 0] = block(far, 0, small)
        pass_on(1, half, 0, 0)
        tx2[half, 1, 0] = block(far, small, part)
        pass_on(1, half, 1, 0)
        tx2[half, 0, 1] = block(right, small, part)
        pass_on(1, half, 0, 1)
        tx2[half, 1, 1] = block(left, 0, small)
        pass_on(1, half, 1, 1)
        tx2[half, 0, 2] = block(right, 0, small)
        tx2[half, 1, 2] = block(left, small, part)
        sum2[half] = block(pos, 0, part)
    for half in range(2):
        for way in range(2):
            sent[1, half, way, 0].wait_recv()
            tx2[half, way, 2] += rx2[half, way, 0]
            pass_on(1, half, way, 2)
    mine_y = []
    for half in range(2):
        for way in range(2):
            sent[1, half, way, 1].wait_recv()
            sent[1, half, way, 2].wait_recv()
        lower = (sum2[half, small:] + (rx2[half, 0, 1] + rx2[half, 1, 2])) * scale
        upper = (sum2[half, :small] + (rx2[half, 1, 1] + rx2[half, 0, 2])) * scale
        yall[half, y, x] = jnp.concatenate([upper, lower], axis=0).astype(BF16)
        mine_y.append(yall[half, y, x])

    def held(half, stage, px, py, lo=None):
        if stage == 0:
            ref = yall.at[half, py, px]
            return ref if lo is None else ref.at[pl.ds(lo * small, small)]
        if half == 0:
            ref = yall.at[half, py]
            return ref if lo is None else ref.at[pl.ds(2 * lo, 2)]
        return yall.at[half, :, px] if lo is None else yall.at[half, pl.ds(2 * lo, 2), px]

    near, relay = {}, {}

    def spread(stage):
        for half in range(2):
            axis = half if stage == 0 else 1 - half
            for way in range(2):
                ref = held(half, stage, x, y)
                near[stage, half, way] = go(ref, ref, "feature", beside(axis, way))

    def spread_far(stage):
        for half in range(2):
            axis = half if stage == 0 else 1 - half
            for way in range(2):
                near[stage, half, way].wait_recv()
                back = lax.rem(here[axis] + (3 if way == 0 else 1), 4)
                px, py = (back, y) if axis == 0 else (x, back)
                ref = held(half, stage, px, py, way)
                relay[stage, half, way] = go(ref, ref, "feature", beside(axis, way))

    def spread_end(stage):
        for half in range(2):
            for way in range(2):
                relay[stage, half, way].wait_recv()

    spread(0)

    ys = jnp.concatenate(mine_y, axis=0)
    yt = ys.T
    nb = k // B
    at = 0
    for i in range(nb):
        row = jnp.dot(yt[i * B : (i + 1) * B], ys[:, : (i + 1) * B], preferred_element_type=F32)
        for j in range(i + 1):
            packed[at * B : (at + 1) * B, :] = row[:, j * B : (j + 1) * B]
            at += 1
    mine = at * B // 2
    share_rows = mine // nf
    base = pl.multiple_of(c * mine, 8)
    other = pl.multiple_of((1 - c) * mine, 8)
    pair = go(packed.at[pl.ds(other, mine)], rx0, "sample", twin)
    spread_far(0)
    pair.wait_recv()
    half_ref[...] = packed[pl.ds(base, mine), :] + rx0[...]

    def share(p):
        return pl.ds(pl.multiple_of(p * share_rows, 8), share_rows)

    got = []
    for d in range(1, nf):
        to = lax.rem(f + d, nf)
        got.append(go(half_ref.at[share(to)], rxp.at[d - 1], "feature", to))
    spread_end(0)
    spread(1)

    def project(half, py, px, first=False):
        if py is None:
            a = [yall[half, j, px] for j in range(4)]
            t = [half * 16 * part + (4 * j + px) * part for j in range(4)]
            b = [slab_ref[pl.ds(pl.multiple_of(i, 16), part), :] for i in t]
            a, b = jnp.concatenate(a, axis=0), jnp.concatenate(b, axis=0)
        else:
            a = yall[half, py].reshape(big, k)
            b = slab_ref[pl.ds(pl.multiple_of(half * 16 * part + py * big, 16), big), :]
        p = lax.dot_general(a, b, (((0,), (0,)), ((), ())), preferred_element_type=F32)
        zacc[...] = p if first else zacc[...] + p

    project(0, y, None, True)
    project(1, None, x)
    for copy in got:
        copy.wait_recv()
    total = half_ref[share(f), :]
    for d in range(1, nf):
        total += rxp[d - 1]
    rxz[z] = total
    got = []
    for d in range(1, nz):
        got.append(go(rxz.at[z], rxz.at[z], "sample", lax.rem(s + 2 * d, 2 * nz)))
    for copy in got:
        copy.wait_recv()
    total = rxz[0]
    for d in range(1, nz):
        total += rxz[d]
    own = pl.ds(pl.multiple_of(base + f * share_rows, 8), share_rows)
    gsum[own, :] = total
    got = []
    for d in range(1, nf):
        got.append(go(gsum.at[own], gsum.at[own], "feature", lax.rem(f + d, nf)))
    spread_far(1)
    for step in (1, 3):
        project(0, lax.rem(y + step, 4), None)
        project(1, None, lax.rem(x + step, 4))
    for copy in got:
        copy.wait_recv()
    whole = pl.ds(base, mine)
    pair = go(gsum.at[whole], gsum.at[whole], "sample", twin)
    spread_end(1)
    project(0, lax.rem(y + 2, 4), None)
    project(1, None, lax.rem(x + 2, 4))

    keep = k // 2
    theirs = go(zacc.at[pl.ds(pl.multiple_of((1 - c) * keep, 8), keep)], rxt, "sample", twin)
    hops = nz // 2
    ring = {}
    for way in range(2):
        to = 2 * lax.rem(z + (1 if way == 0 else nz - 1), nz) + c
        for j in range(hops):
            part_rows = pl.ds(0, keep // 2 if j == 0 else keep)
            ring[way, j] = plan(txr.at[way, j, part_rows], rxr.at[way, j, part_rows], "sample", to)
    mid = keep // 2

    def chunk(pos, lo=0, hi=keep):
        col = pl.ds(pl.multiple_of(pos * B, B), B)
        return zacc[pl.ds(pl.multiple_of(c * keep + lo, 8), hi - lo), col] + rxt[lo:hi, col]

    def hop(j):
        if j == 0:
            theirs.wait_recv()
        for way in range(2):
            pos = lax.rem(z + (hops - j if way == 0 else nz - hops + j), nz)
            lo = way * mid
            if j == 0:
                txr[way, 0, :mid] = chunk(pos, lo, lo + mid)
            else:
                ring[way, j - 1].wait_recv()
                if j == 1:
                    rest = mid - lo
                    txr[way, 1, lo : lo + mid] = chunk(pos, lo, lo + mid) + rxr[way, 0, :mid]
                    txr[way, 1, rest : rest + mid] = chunk(pos, rest, rest + mid)
                else:
                    txr[way, j] = chunk(pos) + rxr[way, j - 1]
            ring[way, j].start()

    ours = pl.ds(pl.multiple_of(c * keep, 8), keep)
    last = plan(zc.at[ours], zc.at[ours], "sample", twin)

    def meet():
        for way in range(2):
            ring[way, hops - 1].wait_recv()
        zc[ours, :] = chunk(z) + (rxr[0, hops - 1] + rxr[1, hops - 1])
        last.start()

    pair.wait_recv()
    n = k
    at = 0
    for i in range(nb):
        for j in range(i + 1):
            tile = gsum[at * B : (at + 1) * B, :]
            w[i * B : (i + 1) * B, j * B : (j + 1) * B] = tile
            if j < i:
                w[j * B : (j + 1) * B, i * B : (i + 1) * B] = tile.T
            at += 1
    out_scale = 1.0 / math.sqrt(tokens)
    inv_ref[...] = jnp.zeros_like(inv_ref)
    factor_ref[...] = jnp.zeros_like(factor_ref)

    def finish(i, low):
        at, end = i * B, (i + 1) * B
        span = slice(at, end)
        rid = lax.broadcasted_iota(jnp.int32, (B, B), 0)
        cid = lax.broadcasted_iota(jnp.int32, (B, B), 1)
        factor_ref[span, span] = jnp.where(cid >= rid, high(low, w[span, span]), 0.0) * out_scale
        inv_ref[span, span] = low
        if at:
            left = high(low, w[span, :at])
            inv_ref[span, :at] = left
        if end < n:
            right = high(low, w[span, end:])
            factor_ref[span, end:] = right * out_scale
            coef = right.T
            w[end:, end:] -= high(coef, right)
            w[end:, span] = -high(coef, low)
            if at:
                w[end:, :at] -= high(coef, left)

    slots = {1: lambda: hop(0), 2: lambda: hop(1), 4: lambda: hop(2), 5: lambda: hop(3), 7: meet}

    def step(i, _):
        at = pl.multiple_of(i * B, B)

        def hook(second):
            for j, work in slots.items():
                if j % 2 == second:
                    pl.when(i == j // 2)(work)

        hook(0)
        rows_here = w[pl.ds(at, B), pl.ds(at, B)].reshape(B // 8, 8, B)
        low = inverse_factor(rows_here, lambda: hook(1))
        for j in range(nb):
            pl.when(i == j)(functools.partial(finish, j, low))
        return 0

    lax.fori_loop(0, nb, step, 0)

    last.wait_recv()
    out_rows = out_ref.shape[0]
    picked = [inv_ref[pl.ds(pl.multiple_of((2 * j + c) * out_rows, 8), out_rows), :] for j in range(nz)]
    cout[...] = high(jnp.concatenate(picked, axis=0), zc[...]).reshape(cout.shape)
    col = pl.ds(pl.multiple_of(z * B, B), B)
    out_ref[:, col] = cout[z]
    got = []
    for d in range(1, nz):
        to = lax.rem(z + d, nz)
        got.append(go(cout.at[to], out_ref.at[:, col], "sample", 2 * to + c))
    for copy in got:
        copy.wait_recv()
    for copy in copies:
        copy.wait_send()


def shards(slab, omega):
    tokens, width = slab.shape
    depth, k = omega.shape
    nf, ns = lax.axis_size("feature"), lax.axis_size("sample")
    nz = ns // 2
    part = tokens // (2 * nf)
    big, cut, small = 4 * part, 2 * part, part // 2
    nb = k // B
    packed = nb * (nb + 1) // 2 * B
    mine = packed // 2
    share = mine // nf
    keep = k // 2
    sems = 24 + 16 + 2 * nf + nz + 4 * (nz // 2) + nz + 8
    return pl.pallas_call(
        functools.partial(kernel, 1.0 / math.sqrt(24.0 * D), tokens * ns),
        out_shape=(jax.ShapeDtypeStruct((k // ns, width), F32), jax.ShapeDtypeStruct((k, k), F32)),
        in_specs=[VMEM, VMEM],
        out_specs=[VMEM, VMEM],
        scratch_shapes=[
            pltpu.VMEM((depth, k), BF16),
            pltpu.VMEM((2, 2, 3, cut, k), BF16),
            pltpu.VMEM((2, 2, 3, cut, k), BF16),
            pltpu.VMEM((2, 2, cut, k), F32),
            pltpu.VMEM((2, big, k), F32),
            pltpu.VMEM((2, 2, 3, small, k), F32),
            pltpu.VMEM((2, 2, 3, small, k), F32),
            pltpu.VMEM((2, part, k), F32),
            pltpu.VMEM((2, 4, 4, part, k), BF16),
            pltpu.VMEM((packed, B), F32),
            pltpu.VMEM((mine, B), F32),
            pltpu.VMEM((mine, B), F32),
            pltpu.VMEM((nf - 1, share, B), F32),
            pltpu.VMEM((nz, share, B), F32),
            pltpu.VMEM((packed, B), F32),
            pltpu.VMEM((k, width), F32),
            pltpu.VMEM((keep, width), F32),
            pltpu.VMEM((2, nz // 2, keep, B), F32),
            pltpu.VMEM((2, nz // 2, keep, B), F32),
            pltpu.VMEM((k, B), F32),
            pltpu.VMEM((nz, k // ns, B), F32),
            pltpu.VMEM((k, k), F32),
            pltpu.VMEM((k, k), F32),
            pltpu.SemaphoreType.DMA((sems,)),
            pltpu.SemaphoreType.DMA((sems,)),
        ],
        compiler_params=pltpu.CompilerParams(collective_id=0, has_side_effects=True, vmem_limit_bytes=56 * MIB),
        name="range_finder",
    )(slab, omega)


def solution(mesh):
    placed = (P("sample", "feature"), P("feature", None))
    return jax.shard_map(
        shards, mesh=mesh, in_specs=placed, out_specs=(P("sample", "feature"), P()), check_vma=False
    )
```

```python
import functools
import math

import jax
import jax.numpy as jnp
from jax import lax
from jax.experimental import pallas as pl
from jax.experimental.pallas import tpu as pltpu
from jax.sharding import PartitionSpec as P

D = 16384
F32 = jnp.float32
BF16 = jnp.bfloat16
HIGH = lax.Precision.HIGHEST
MIB = 1 << 20
B = 128
VMEM = pl.BlockSpec(memory_space=pltpu.VMEM)
HBM = pl.BlockSpec(memory_space=pl.ANY)


def remote(src, dst, send_sem, recv_sem, axis, index):
    return pltpu.make_async_remote_copy(
        src_ref=src,
        dst_ref=dst,
        send_sem=send_sem,
        recv_sem=recv_sem,
        device_id={axis: index},
        device_id_type=pl.DeviceIdType.MESH,
    )


def greet(barrier, axis, index):
    pl.semaphore_signal(barrier, inc=1, device_id={axis: index}, device_id_type=pl.DeviceIdType.MESH)


def rep(a):
    return jnp.broadcast_to(a, a.shape[:-2] + (8, 128))


def inverse_factor(s, rows, hook):
    n = s.shape[0]
    sub = lax.broadcasted_iota(jnp.int32, (8, 128), 0)
    lane = lax.broadcasted_iota(jnp.int32, (8, 128), 1)
    s = [s[q] for q in range(n)]
    x = [jnp.where(sub + 8 * q == lane, 1.0, 0.0) for q in range(n)]
    out = []
    for p in range(n):
        if p and p % (n // 4) == 0:
            hook(p // (n // 4))
        cols = [rep(s[p][:, 8 * p + c : 8 * p + c + 1]) for c in range(8)]
        for c in range(8):
            rows[c] = cols[c]
        rows[8] = s[p]
        rows[9] = x[p]
        e = {(r, c): rep(rows[c, r : r + 1]) for c in range(8) for r in range(c, 8)}
        rg = [rep(rows[8, r : r + 1]) for r in range(8)]
        rx = [rep(rows[9, r : r + 1]) for r in range(8)]
        m, wg, wx = {}, [None] * 8, [None] * 8
        for r in range(0, 8, 2):
            a, b, d = e[r, r], e[r + 1, r], e[r + 1, r + 1]
            idet = 1.0 / (a * d - b * b)
            ia = 1.0 / a
            for t in range(r + 2, 8):
                m[t, r] = (e[t, r] * d - e[t, r + 1] * b) * idet
                m[t, r + 1] = (e[t, r + 1] * a - e[t, r] * b) * idet
            for t in range(r + 2, 8):
                for c in range(r + 2, t + 1):
                    e[t, c] = e[t, c] - (m[t, r] * e[c, r] + m[t, r + 1] * e[c, r + 1])
            for t in range(r + 2, 8):
                rg[t] = rg[t] - (m[t, r] * rg[r] + m[t, r + 1] * rg[r + 1])
                rx[t] = rx[t] - (m[t, r] * rx[r] + m[t, r + 1] * rx[r + 1])
            for v, w in ((rg, wg), (rx, wx)):
                w[r] = (v[r] * d - v[r + 1] * b) * idet
                w[r + 1] = (v[r + 1] * a - v[r] * b) * idet
            o0 = rx[r] * lax.rsqrt(a)
            o1 = (rx[r + 1] - (b * ia) * rx[r]) * lax.rsqrt((a * d - b * b) * ia)
            ox = o0 if r == 0 else jnp.where(sub == r, o0, ox)
            ox = jnp.where(sub == r + 1, o1, ox)
        out.append(ox)
        if p + 1 < n:
            for r in range(6, 0, -2):
                for t in range(r):
                    wg[t] = wg[t] - (m[r, t] * wg[r] + m[r + 1, t] * wg[r + 1])
                    wx[t] = wx[t] - (m[r, t] * wx[r] + m[r + 1, t] * wx[r + 1])
            for q in range(p + 1, n):
                k = [rep(s[q][:, 8 * p + c : 8 * p + c + 1]) for c in range(8)]
                for w, v in ((wg, s), (wx, x)):
                    t = [k[c] * w[c] for c in range(8)]
                    v[q] = v[q] - (((t[0] + t[1]) + (t[2] + t[3])) + ((t[4] + t[5]) + (t[6] + t[7])))
    return jnp.concatenate(out, axis=0)


def high(a, b):
    return jnp.dot(a, b, precision=HIGH, preferred_element_type=F32)


def kernel(
    scale, tokens, slab_hbm, omega_hbm, out_ref, factor_hbm,
    slab_ref, omega_ref, factor_ref, load_sem, wide, tx1, rx1, side1, own1, tx2, rx2, sum2,
    yall, packed, rx0, half_ref, rxp, rxz, gsum,
    zacc, rxt, txr, rxr, zc, cout, w, row_ref, inv_ref, send_sem, recv_sem,
):
    f, s = lax.axis_index("feature"), lax.axis_index("sample")
    nf, nz = lax.axis_size("feature"), lax.axis_size("sample") // 2
    x, y = lax.rem(f, 4), f // 4
    z, c = s // 2, lax.rem(s, 2)
    twin = 2 * z + 1 - c
    barrier = pltpu.get_barrier_semaphore()
    greet(barrier, "sample", twin)
    for d in range(1, nf):
        greet(barrier, "feature", lax.rem(f + d, nf))
    for d in range(1, nz):
        greet(barrier, "sample", lax.rem(s + 2 * d, 2 * nz))

    loads = {}
    here = (lax.rem(f, 4), f // 4)

    def load(n, src, dst):
        loads[n] = pltpu.make_async_copy(src, dst, load_sem.at[len(loads)])
        loads[n].start()

    def tokens_of(ref, half, pos):
        return ref.at[half, :, pos] if half == 0 else ref.at[half, pos]

    load("omega", omega_hbm, omega_ref)
    for step in (2, 1, 3, 0):
        for half in range(2):
            pos = lax.rem(here[half] + step, 4)
            load((half, step), tokens_of(slab_hbm, half, pos), tokens_of(slab_ref, half, pos))

    copies = []
    count = [0]

    def plan(src, dst, axis, to):
        n = count[0]
        count[0] += 1
        copy = remote(src, dst, send_sem.at[n], recv_sem.at[n], axis, to)
        copies.append(copy)
        return copy

    def go(src, dst, axis, to):
        copy = plan(src, dst, axis, to)
        copy.start()
        return copy

    def node(axis, pos):
        return 4 * y + pos if axis == 0 else 4 * pos + x

    def beside(axis, way):
        return node(axis, lax.rem(here[axis] + (1 if way == 0 else 3), 4))

    loads["omega"].wait()
    wide[...] = omega_ref[...].astype(BF16)
    part = yall.shape[3]
    k = yall.shape[4]
    big = 4 * part
    cut = big // 2
    small = part // 2

    def product(half, step):
        loads[half, step].wait()
        a = tokens_of(slab_ref, half, lax.rem(here[half] + step, 4))[...].reshape(big, -1)
        return jnp.dot(a, wide[...], preferred_element_type=F32)

    sent = {}

    def pass_on(stage, half, way, piece):
        axis = half if stage == 0 else 1 - half
        tx, rx = (tx1, rx1) if stage == 0 else (tx2, rx2)
        sent[stage, half, way, piece] = go(
            tx.at[half, way, piece], rx.at[half, way, piece], "feature", beside(axis, way)
        )

    for half in range(2):
        far = product(half, 2).astype(BF16)
        tx1[half, 0, 0] = far[:cut]
        tx1[half, 1, 0] = far[cut:]
        if half == 0:
            pl.semaphore_wait(barrier, nf + nz - 1)
        pass_on(0, half, 0, 0)
        pass_on(0, half, 1, 0)
    for half in range(2):
        right = product(half, 1)
        tx1[half, 0, 1] = right[cut:].astype(BF16)
        pass_on(0, half, 0, 1)
        side1[half, 0] = right[:cut]
        left = product(half, 3)
        tx1[half, 1, 1] = left[:cut].astype(BF16)
        pass_on(0, half, 1, 1)
        side1[half, 1] = left[cut:]
    for half in range(2):
        for way in range(2):
            sent[0, half, way, 0].wait_recv()
            tx1[half, way, 2] = (side1[half, way] + rx1[half, way, 0].astype(F32)).astype(BF16)
            pass_on(0, half, way, 2)
    for half in range(2):
        own1[half] = product(half, 0)
    for half in range(2):
        for way in range(2):
            sent[0, half, way, 1].wait_recv()
        own1[half, cut:] += rx1[half, 0, 1].astype(F32)
        own1[half, :cut] += rx1[half, 1, 1].astype(F32)
        for way in range(2):
            sent[0, half, way, 2].wait_recv()
        own1[half, :cut] += rx1[half, 0, 2].astype(F32)
        own1[half, cut:] += rx1[half, 1, 2].astype(F32)

        def block(pos, lo, hi):
            return own1[half, pl.ds(pl.multiple_of(pos * part + lo, 8), hi - lo), :]

        pos = here[1 - half]
        far, right, left = (lax.rem(pos + step, 4) for step in (2, 1, 3))
        tx2[half, 0, 0] = block(far, 0, small)
        pass_on(1, half, 0, 0)
        tx2[half, 1, 0] = block(far, small, part)
        pass_on(1, half, 1, 0)
        tx2[half, 0, 1] = block(right, small, part)
        pass_on(1, half, 0, 1)
        tx2[half, 1, 1] = block(left, 0, small)
        pass_on(1, half, 1, 1)
        tx2[half, 0, 2] = block(right, 0, small)
        tx2[half, 1, 2] = block(left, small, part)
        sum2[half] = block(pos, 0, part)
    for half in range(2):
        for way in range(2):
            sent[1, half, way, 0].wait_recv()
            tx2[half, way, 2] += rx2[half, way, 0]
            pass_on(1, half, way, 2)
    mine_y = []
    for half in range(2):
        for way in range(2):
            sent[1, half, way, 1].wait_recv()
            sent[1, half, way, 2].wait_recv()
        lower = (sum2[half, small:] + (rx2[half, 0, 1] + rx2[half, 1, 2])) * scale
        upper = (sum2[half, :small] + (rx2[half, 1, 1] + rx2[half, 0, 2])) * scale
        yall[half, y, x] = jnp.concatenate([upper, lower], axis=0).astype(BF16)
        mine_y.append(yall[half, y, x])

    def held(half, stage, px, py, lo=None):
        if stage == 0:
            ref = yall.at[half, py, px]
            return ref if lo is None else ref.at[pl.ds(lo * small, small)]
        if half == 0:
            ref = yall.at[half, py]
            return ref if lo is None else ref.at[pl.ds(2 * lo, 2)]
        return yall.at[half, :, px] if lo is None else yall.at[half, pl.ds(2 * lo, 2), px]

    near, relay = {}, {}

    def spread(stage):
        for half in range(2):
            axis = half if stage == 0 else 1 - half
            for way in range(2):
                ref = held(half, stage, x, y)
                near[stage, half, way] = go(ref, ref, "feature", beside(axis, way))

    def spread_far(stage):
        for half in range(2):
            axis = half if stage == 0 else 1 - half
            for way in range(2):
                near[stage, half, way].wait_recv()
                back = lax.rem(here[axis] + (3 if way == 0 else 1), 4)
                px, py = (back, y) if axis == 0 else (x, back)
                ref = held(half, stage, px, py, way)
                relay[stage, half, way] = go(ref, ref, "feature", beside(axis, way))

    def spread_end(stage):
        for half in range(2):
            for way in range(2):
                relay[stage, half, way].wait_recv()

    spread(0)

    ys = jnp.concatenate(mine_y, axis=0)
    yt = ys.T
    nb = k // B
    at = 0
    for i in range(nb):
        row = jnp.dot(yt[i * B : (i + 1) * B], ys[:, : (i + 1) * B], preferred_element_type=F32)
        for j in range(i + 1):
            packed[at * B : (at + 1) * B, :] = row[:, j * B : (j + 1) * B]
            at += 1
    mine = at * B // 2
    share_rows = mine // nf
    base = pl.multiple_of(c * mine, 8)
    other = pl.multiple_of((1 - c) * mine, 8)
    pair = go(packed.at[pl.ds(other, mine)], rx0, "sample", twin)
    spread_far(0)
    pair.wait_recv()
    half_ref[...] = packed[pl.ds(base, mine), :] + rx0[...]

    def share(p):
        return pl.ds(pl.multiple_of(p * share_rows, 8), share_rows)

    got = []
    for d in range(1, nf):
        to = lax.rem(f + d, nf)
        got.append(go(half_ref.at[share(to)], rxp.at[d - 1], "feature", to))
    spread_end(0)
    spread(1)

    def project(*steps):
        a, b = [], []
        for step in steps:
            row, col = lax.rem(y + step, 4), lax.rem(x + step, 4)
            a += [yall[0, row].reshape(big, k), yall[1, :, col].reshape(big, k)]
            b += [slab_ref[0, row].reshape(big, -1), slab_ref[1, :, col].reshape(big, -1)]
        a, b = jnp.concatenate(a, axis=0), jnp.concatenate(b, axis=0)
        p = lax.dot_general(a, b, (((0,), (0,)), ((), ())), preferred_element_type=F32)
        zacc[...] = p if steps == (0,) else zacc[...] + p

    project(0)
    for copy in got:
        copy.wait_recv()
    total = half_ref[share(f), :]
    for d in range(1, nf):
        total += rxp[d - 1]
    rxz[z] = total
    got = []
    for d in range(1, nz):
        got.append(go(rxz.at[z], rxz.at[z], "sample", lax.rem(s + 2 * d, 2 * nz)))
    for copy in got:
        copy.wait_recv()
    total = rxz[0]
    for d in range(1, nz):
        total += rxz[d]
    own = pl.ds(pl.multiple_of(base + f * share_rows, 8), share_rows)
    gsum[own, :] = total
    got = []
    for d in range(1, nf):
        got.append(go(gsum.at[own], gsum.at[own], "feature", lax.rem(f + d, nf)))
    spread_far(1)
    project(1, 3)
    for copy in got:
        copy.wait_recv()
    whole = pl.ds(base, mine)
    pair = go(gsum.at[whole], gsum.at[whole], "sample", twin)

    keep = k // 2
    hops = nz // 2

    def columns(pos):
        return pl.ds(pl.multiple_of(pos * B, B), B)

    order = sorted(range(nz), key=lambda d: -min(d, nz - d))
    theirs = {}
    for d in order:
        col = columns(lax.rem(z + d, nz))
        theirs[d] = plan(
            zacc.at[pl.ds(pl.multiple_of((1 - c) * keep, 8), keep), col], rxt.at[:, col], "sample", twin
        )

    def finish_product():
        spread_end(1)
        project(2)
        for d in order:
            theirs[d].start()

    ring = {}
    for way in range(2):
        to = 2 * lax.rem(z + (1 if way == 0 else nz - 1), nz) + c
        for j in range(hops):
            part_rows = pl.ds(0, keep // 2 if j == 0 else keep)
            ring[way, j] = plan(txr.at[way, j, part_rows], rxr.at[way, j, part_rows], "sample", to)
    mid = keep // 2

    def chunk(pos, lo=0, hi=keep):
        col = columns(pos)
        return zacc[pl.ds(pl.multiple_of(c * keep + lo, 8), hi - lo), col] + rxt[lo:hi, col]

    def hop(j):
        for way in range(2):
            d = hops - j if way == 0 else nz - hops + j
            pos = lax.rem(z + d, nz)
            if j or way == 0:
                theirs[d].wait_recv()
            lo = way * mid
            if j == 0:
                txr[way, 0, :mid] = chunk(pos, lo, lo + mid)
            else:
                ring[way, j - 1].wait_recv()
                if j == 1:
                    rest = mid - lo
                    txr[way, 1, lo : lo + mid] = chunk(pos, lo, lo + mid) + rxr[way, 0, :mid]
                    txr[way, 1, rest : rest + mid] = chunk(pos, rest, rest + mid)
                else:
                    txr[way, j] = chunk(pos) + rxr[way, j - 1]
            ring[way, j].start()

    ours = pl.ds(pl.multiple_of(c * keep, 8), keep)
    last = plan(zc.at[ours], zc.at[ours], "sample", twin)

    def meet():
        theirs[0].wait_recv()
        for way in range(2):
            ring[way, hops - 1].wait_recv()
        zc[ours, :] = chunk(z) + (rxr[0, hops - 1] + rxr[1, hops - 1])
        last.start()

    pair.wait_recv()
    n = k
    rid = lax.broadcasted_iota(jnp.int32, (B, B), 0)
    cid = lax.broadcasted_iota(jnp.int32, (B, B), 1)
    top = jnp.zeros((B, B), F32)
    for i in range(nb):
        last_of_row = (i + 1) * (i + 2) // 2 * B
        top = jnp.maximum(top, gsum[last_of_row - B : last_of_row, :])
    top = jnp.max(jnp.where(rid == cid, top, 0.0), axis=(0, 1), keepdims=True)
    unit = lax.rsqrt(top)
    at = 0
    for i in range(nb):
        for j in range(i + 1):
            tile = gsum[at * B : (at + 1) * B, :] * (unit * unit)
            w[i * B : (i + 1) * B, j * B : (j + 1) * B] = tile
            if j < i:
                w[j * B : (j + 1) * B, i * B : (i + 1) * B] = tile.T
            at += 1
    out_scale = (1.0 / math.sqrt(tokens)) / unit
    inv_ref[...] = jnp.zeros_like(inv_ref)
    factor_ref[...] = jnp.zeros_like(factor_ref)

    def finish(i, low):
        at, end = i * B, (i + 1) * B
        span = slice(at, end)
        factor_ref[span, span] = jnp.where(cid >= rid, high(low, w[span, span]), 0.0) * out_scale
        inv_ref[span, span] = low
        if at:
            left = high(low, w[span, :at])
            inv_ref[span, :at] = left
        if end < n:
            right = high(low, w[span, end:])
            factor_ref[span, end:] = right * out_scale
            coef = right.T
            w[end:, end:] -= high(coef, right)
            w[end:, span] = -high(coef, low)
            if at:
                w[end:, :at] -= high(coef, left)

    slots = {
        1: finish_product,
        2: lambda: hop(0),
        4: lambda: hop(1),
        7: lambda: hop(2),
        10: lambda: hop(3),
        13: meet,
    }

    def step(i, _):
        at = pl.multiple_of(i * B, B)

        def hook(quarter):
            for j, work in slots.items():
                if j % 4 == quarter:
                    pl.when(i == j // 4)(work)

        hook(0)
        rows_here = w[pl.ds(at, B), pl.ds(at, B)].reshape(B // 8, 8, B)
        low = inverse_factor(rows_here, row_ref, hook)
        for j in range(nb):
            pl.when(i == j)(functools.partial(finish, j, low))
        return 0

    lax.fori_loop(0, nb, step, 0)

    store = pltpu.make_async_copy(factor_ref, factor_hbm, load_sem.at[len(loads)])
    store.start()

    last.wait_recv()
    out_rows = out_ref.shape[0]
    picked = [inv_ref[pl.ds(pl.multiple_of((2 * j + c) * out_rows, 8), out_rows), :] for j in range(nz)]
    cout[...] = (high(jnp.concatenate(picked, axis=0), zc[...]) * unit).reshape(cout.shape)
    col = columns(z)
    out_ref[:, col] = cout[z]
    got = []
    for d in range(1, nz):
        to = lax.rem(z + d, nz)
        got.append(go(cout.at[to], out_ref.at[:, col], "sample", 2 * to + c))
    for copy in got:
        copy.wait_recv()
    for copy in copies:
        copy.wait_send()
    store.wait()


def hand_over(a_ref, b_ref, a_out, b_out, sem):
    copies = [pltpu.make_async_copy(a_ref, a_out, sem.at[4])]
    rows = b_ref.shape[0] // 4
    for j in range(4):
        part = pl.ds(j * rows, rows)
        copies.append(pltpu.make_async_copy(b_ref.at[part], b_out.at[part], sem.at[j]))
    for copy in copies:
        copy.start()
    for copy in copies:
        copy.wait()


def shards(slab, omega):
    tokens, width = slab.shape
    depth, k = omega.shape
    nf, ns = lax.axis_size("feature"), lax.axis_size("sample")
    nz = ns // 2
    part = tokens // (2 * nf)
    big, cut, small = 4 * part, 2 * part, part // 2
    nb = k // B
    packed = nb * (nb + 1) // 2 * B
    mine = packed // 2
    share = mine // nf
    keep = k // 2
    sems = 24 + 16 + 2 * nf + 2 * nz + 4 * (nz // 2) + nz + 8
    found = pl.pallas_call(
        functools.partial(kernel, 1.0 / math.sqrt(24.0 * D), tokens * ns),
        out_shape=(jax.ShapeDtypeStruct((k // ns, width), F32), jax.ShapeDtypeStruct((k, k), F32)),
        in_specs=[HBM, HBM],
        out_specs=[VMEM, HBM],
        scratch_shapes=[
            pltpu.VMEM((2, 4, 4, part, width), BF16),
            pltpu.VMEM((depth, k), omega.dtype),
            pltpu.VMEM((k, k), F32),
            pltpu.SemaphoreType.DMA((10,)),
            pltpu.VMEM((depth, k), BF16),
            pltpu.VMEM((2, 2, 3, cut, k), BF16),
            pltpu.VMEM((2, 2, 3, cut, k), BF16),
            pltpu.VMEM((2, 2, cut, k), F32),
            pltpu.VMEM((2, big, k), F32),
            pltpu.VMEM((2, 2, 3, small, k), F32),
            pltpu.VMEM((2, 2, 3, small, k), F32),
            pltpu.VMEM((2, part, k), F32),
            pltpu.VMEM((2, 4, 4, part, k), BF16),
            pltpu.VMEM((packed, B), F32),
            pltpu.VMEM((mine, B), F32),
            pltpu.VMEM((mine, B), F32),
            pltpu.VMEM((nf - 1, share, B), F32),
            pltpu.VMEM((nz, share, B), F32),
            pltpu.VMEM((packed, B), F32),
            pltpu.VMEM((k, width), F32),
            pltpu.VMEM((keep, width), F32),
            pltpu.VMEM((2, nz // 2, keep, B), F32),
            pltpu.VMEM((2, nz // 2, keep, B), F32),
            pltpu.VMEM((k, B), F32),
            pltpu.VMEM((nz, k // ns, B), F32),
            pltpu.VMEM((k, k), F32),
            pltpu.VMEM((10, 8, B), F32),
            pltpu.VMEM((k, k), F32),
            pltpu.SemaphoreType.DMA((sems,)),
            pltpu.SemaphoreType.DMA((sems,)),
        ],
        compiler_params=pltpu.CompilerParams(collective_id=0, has_side_effects=True, vmem_limit_bytes=56 * MIB),
        name="range_finder",
    )(slab.reshape(2, 4, 4, part, width), omega)
    return pl.pallas_call(
        hand_over,
        out_shape=tuple(jax.ShapeDtypeStruct(a.shape, a.dtype) for a in found),
        in_specs=[HBM, HBM],
        out_specs=[HBM, HBM],
        scratch_shapes=[pltpu.SemaphoreType.DMA((5,))],
        compiler_params=pltpu.CompilerParams(vmem_limit_bytes=56 * MIB),
        name="hand_over",
    )(*found)


def solution(mesh):
    placed = (P("sample", "feature"), P("feature", None))
    return jax.shard_map(
        shards, mesh=mesh, in_specs=placed, out_specs=(P("sample", "feature"), P()), check_vma=False
    )
```

```python
import functools
import math

import jax
import jax.numpy as jnp
from jax import lax
from jax.experimental import pallas as pl
from jax.experimental.pallas import tpu as pltpu
from jax.sharding import PartitionSpec as P

D = 16384
F32 = jnp.float32
BF16 = jnp.bfloat16
HIGH = lax.Precision.HIGHEST
MIB = 1 << 20
B = 128
VMEM = pl.BlockSpec(memory_space=pltpu.VMEM)
HBM = pl.BlockSpec(memory_space=pl.ANY)


def remote(src, dst, send_sem, recv_sem, axis, index):
    return pltpu.make_async_remote_copy(
        src_ref=src,
        dst_ref=dst,
        send_sem=send_sem,
        recv_sem=recv_sem,
        device_id={axis: index},
        device_id_type=pl.DeviceIdType.MESH,
    )


def greet(barrier, axis, index):
    pl.semaphore_signal(barrier, inc=1, device_id={axis: index}, device_id_type=pl.DeviceIdType.MESH)


def rep(a):
    return jnp.broadcast_to(a, a.shape[:-2] + (8, 128))


def inverse_factor(s, rows, hook):
    n = s.shape[0]
    sub = lax.broadcasted_iota(jnp.int32, (8, 128), 0)
    lane = lax.broadcasted_iota(jnp.int32, (8, 128), 1)
    s = [s[q] for q in range(n)]
    x = [jnp.where(sub + 8 * q == lane, 1.0, 0.0) for q in range(n)]
    out = []
    for p in range(n):
        if p and p % (n // 4) == 0:
            hook(p // (n // 4))
        cols = [rep(s[p][:, 8 * p + c : 8 * p + c + 1]) for c in range(8)]
        for c in range(8):
            rows[c] = cols[c]
        rows[8] = s[p]
        rows[9] = x[p]
        e = {(r, c): rep(rows[c, r : r + 1]) for c in range(8) for r in range(c, 8)}
        rg = [rep(rows[8, r : r + 1]) for r in range(8)]
        rx = [rep(rows[9, r : r + 1]) for r in range(8)]
        m, wg, wx = {}, [None] * 8, [None] * 8
        for r in range(0, 8, 2):
            a, b, d = e[r, r], e[r + 1, r], e[r + 1, r + 1]
            idet = 1.0 / (a * d - b * b)
            ia = 1.0 / a
            for t in range(r + 2, 8):
                m[t, r] = (e[t, r] * d - e[t, r + 1] * b) * idet
                m[t, r + 1] = (e[t, r + 1] * a - e[t, r] * b) * idet
            for t in range(r + 2, 8):
                for c in range(r + 2, t + 1):
                    e[t, c] = e[t, c] - (m[t, r] * e[c, r] + m[t, r + 1] * e[c, r + 1])
            for t in range(r + 2, 8):
                rg[t] = rg[t] - (m[t, r] * rg[r] + m[t, r + 1] * rg[r + 1])
                rx[t] = rx[t] - (m[t, r] * rx[r] + m[t, r + 1] * rx[r + 1])
            for v, w in ((rg, wg), (rx, wx)):
                w[r] = (v[r] * d - v[r + 1] * b) * idet
                w[r + 1] = (v[r + 1] * a - v[r] * b) * idet
            o0 = rx[r] * lax.rsqrt(a)
            o1 = (rx[r + 1] - (b * ia) * rx[r]) * lax.rsqrt((a * d - b * b) * ia)
            ox = o0 if r == 0 else jnp.where(sub == r, o0, ox)
            ox = jnp.where(sub == r + 1, o1, ox)
        out.append(ox)
        if p + 1 < n:
            for r in range(6, 0, -2):
                for t in range(r):
                    wg[t] = wg[t] - (m[r, t] * wg[r] + m[r + 1, t] * wg[r + 1])
                    wx[t] = wx[t] - (m[r, t] * wx[r] + m[r + 1, t] * wx[r + 1])
            for q in range(p + 1, n):
                k = [rep(s[q][:, 8 * p + c : 8 * p + c + 1]) for c in range(8)]
                for w, v in ((wg, s), (wx, x)):
                    t = [k[c] * w[c] for c in range(8)]
                    v[q] = v[q] - (((t[0] + t[1]) + (t[2] + t[3])) + ((t[4] + t[5]) + (t[6] + t[7])))
    return jnp.concatenate(out, axis=0)


def high(a, b):
    return jnp.dot(a, b, precision=HIGH, preferred_element_type=F32)


def kernel(
    scale, tokens, slab_hbm, omega_hbm, out_ref, factor_hbm,
    slab_ref, omega_ref, factor_ref, load_sem, wide, tx1, rx1, side1, own1, tx2, rx2, sum2,
    yall, packed, rx0, half_ref, rxp, line_ref, rxq, rxz, gsum,
    zacc, rxt, txr, rxr, zc, cout, w, row_ref, inv_ref, send_sem, recv_sem, token_sem,
):
    f, s = lax.axis_index("feature"), lax.axis_index("sample")
    nf, nz = lax.axis_size("feature"), lax.axis_size("sample") // 2
    x, y = lax.rem(f, 4), f // 4
    z, c = s // 2, lax.rem(s, 2)
    twin = 2 * z + 1 - c
    barrier = pltpu.get_barrier_semaphore()
    up, down = 2 * lax.rem(z + 1, nz) + c, 2 * lax.rem(z + nz - 1, nz) + c
    greet(barrier, "sample", twin)
    for d in (1, 3):
        greet(barrier, "feature", 4 * y + lax.rem(x + d, 4))
        greet(barrier, "feature", 4 * lax.rem(y + d, 4) + x)
    for to in (up, down):
        greet(barrier, "sample", to)

    def token(n):
        if n:
            pl.semaphore_wait(token_sem.at[n - 1], 2)
        if n < nz // 2 - 1:
            for to in (up, down):
                greet(token_sem.at[n], "sample", to)

    loads = {}
    here = (lax.rem(f, 4), f // 4)

    def load(n, src, dst):
        loads[n] = pltpu.make_async_copy(src, dst, load_sem.at[len(loads)])
        loads[n].start()

    def tokens_of(ref, half, pos):
        return ref.at[half, :, pos] if half == 0 else ref.at[half, pos]

    load("omega", omega_hbm, omega_ref)
    for step in (2, 1, 3, 0):
        for half in range(2):
            pos = lax.rem(here[half] + step, 4)
            load((half, step), tokens_of(slab_hbm, half, pos), tokens_of(slab_ref, half, pos))
    ready = set()

    copies = []
    count = [0]

    def plan(src, dst, axis, to):
        n = count[0]
        count[0] += 1
        copy = remote(src, dst, send_sem.at[n], recv_sem.at[n], axis, to)
        copies.append(copy)
        return copy

    def go(src, dst, axis, to):
        copy = plan(src, dst, axis, to)
        copy.start()
        return copy

    def node(axis, pos):
        return 4 * y + pos if axis == 0 else 4 * pos + x

    def beside(axis, way):
        return node(axis, lax.rem(here[axis] + (1 if way == 0 else 3), 4))

    loads["omega"].wait()
    wide[...] = omega_ref[...].astype(BF16)
    part = yall.shape[3]
    k = yall.shape[4]
    big = 4 * part
    small = part // 2
    bit = part // 2
    cut = 2 * bit
    fine = bit // 2
    units = [(half, batch) for batch in range(2) for half in range(2)]

    def product(half, batch, step):
        if (half, step) not in ready:
            ready.add((half, step))
            loads[half, step].wait()
        pos = lax.rem(here[half] + step, 4)
        lines = pl.ds(batch * bit, bit)
        a = slab_ref[0, :, pos, lines] if half == 0 else slab_ref[1, pos, :, lines]
        return jnp.dot(a.reshape(4 * bit, -1), wide[...], preferred_element_type=F32)

    sent = {}

    def pass_on(stage, u, way, piece):
        half = units[u][0]
        axis = half if stage == 0 else 1 - half
        tx, rx = (tx1, rx1) if stage == 0 else (tx2, rx2)
        sent[stage, u, way, piece] = go(tx.at[u, way, piece], rx.at[u, way, piece], "feature", beside(axis, way))

    for batch in range(2):
        now = (2 * batch, 2 * batch + 1)
        for u in now:
            far = product(*units[u], 2).astype(BF16)
            tx1[u, 0, 0] = far[:cut]
            tx1[u, 1, 0] = far[cut:]
            if u == 0:
                pl.semaphore_wait(barrier, 7)
                token(0)
            pass_on(0, u, 0, 0)
            pass_on(0, u, 1, 0)
        for u in now:
            right = product(*units[u], 1)
            tx1[u, 0, 1] = right[cut:].astype(BF16)
            pass_on(0, u, 0, 1)
            side1[u, 0] = right[:cut]
            left = product(*units[u], 3)
            tx1[u, 1, 1] = left[:cut].astype(BF16)
            pass_on(0, u, 1, 1)
            side1[u, 1] = left[cut:]
        for u in now:
            for way in range(2):
                sent[0, u, way, 0].wait_recv()
                tx1[u, way, 2] = (side1[u, way] + rx1[u, way, 0].astype(F32)).astype(BF16)
                pass_on(0, u, way, 2)
        token(1 + batch)
    for u in range(4):
        own1[u] = product(*units[u], 0)
    for u in range(4):
        half = units[u][0]
        for way in range(2):
            sent[0, u, way, 1].wait_recv()
        own1[u, cut:] += rx1[u, 0, 1].astype(F32)
        own1[u, :cut] += rx1[u, 1, 1].astype(F32)
        for way in range(2):
            sent[0, u, way, 2].wait_recv()
        own1[u, :cut] += rx1[u, 0, 2].astype(F32)
        own1[u, cut:] += rx1[u, 1, 2].astype(F32)

        def block(pos, lo, hi):
            return own1[u, pl.ds(pl.multiple_of(pos * bit + lo, 8), hi - lo), :]

        pos = here[1 - half]
        far, right, left = (lax.rem(pos + step, 4) for step in (2, 1, 3))
        tx2[u, 0, 0] = block(far, 0, fine)
        pass_on(1, u, 0, 0)
        tx2[u, 1, 0] = block(far, fine, bit)
        pass_on(1, u, 1, 0)
        tx2[u, 0, 1] = block(right, fine, bit)
        pass_on(1, u, 0, 1)
        tx2[u, 1, 1] = block(left, 0, fine)
        pass_on(1, u, 1, 1)
        tx2[u, 0, 2] = block(right, 0, fine)
        tx2[u, 1, 2] = block(left, fine, bit)
        sum2[u] = block(pos, 0, bit)
    for u in range(4):
        for way in range(2):
            sent[1, u, way, 0].wait_recv()
            tx2[u, way, 2] += rx2[u, way, 0]
            pass_on(1, u, way, 2)
    for u in range(4):
        half, batch = units[u]
        for way in range(2):
            sent[1, u, way, 1].wait_recv()
            sent[1, u, way, 2].wait_recv()
        lower = (sum2[u, fine:] + (rx2[u, 0, 1] + rx2[u, 1, 2])) * scale
        upper = (sum2[u, :fine] + (rx2[u, 1, 1] + rx2[u, 0, 2])) * scale
        yall[half, y, x, batch * bit : (batch + 1) * bit] = jnp.concatenate([upper, lower], axis=0).astype(BF16)
    mine_y = [yall[half, y, x] for half in range(2)]

    def held(half, stage, px, py, lo=None):
        if stage == 0:
            ref = yall.at[half, py, px]
            return ref if lo is None else ref.at[pl.ds(lo * small, small)]
        if half == 0:
            ref = yall.at[half, py]
            return ref if lo is None else ref.at[pl.ds(2 * lo, 2)]
        return yall.at[half, :, px] if lo is None else yall.at[half, pl.ds(2 * lo, 2), px]

    near, relay = {}, {}

    def spread(stage):
        for half in range(2):
            axis = half if stage == 0 else 1 - half
            for way in range(2):
                ref = held(half, stage, x, y)
                near[stage, half, way] = go(ref, ref, "feature", beside(axis, way))

    def spread_far(stage):
        for half in range(2):
            axis = half if stage == 0 else 1 - half
            for way in range(2):
                near[stage, half, way].wait_recv()
                back = lax.rem(here[axis] + (3 if way == 0 else 1), 4)
                px, py = (back, y) if axis == 0 else (x, back)
                ref = held(half, stage, px, py, way)
                relay[stage, half, way] = go(ref, ref, "feature", beside(axis, way))

    def spread_end(stage):
        for half in range(2):
            for way in range(2):
                relay[stage, half, way].wait_recv()

    spread(0)

    ys = jnp.concatenate(mine_y, axis=0)
    yt = ys.T
    nb = k // B
    at = 0
    for i in range(nb):
        row = jnp.dot(yt[i * B : (i + 1) * B], ys[:, : (i + 1) * B], preferred_element_type=F32)
        for j in range(i + 1):
            packed[at * B : (at + 1) * B, :] = row[:, j * B : (j + 1) * B]
            at += 1
    mine = at * B // 2
    share_rows = mine // nf
    base = pl.multiple_of(c * mine, 8)
    other = pl.multiple_of((1 - c) * mine, 8)
    pair = go(packed.at[pl.ds(other, mine)], rx0, "sample", twin)
    spread_far(0)
    pair.wait_recv()
    half_ref[...] = packed[pl.ds(base, mine), :] + rx0[...]

    line = 4 * share_rows
    first, second = x + c * (y - x), y + c * (x - y)

    def partner(axis, d):
        along_y = c if axis == 0 else 1 - c
        return 4 * lax.rem(y + d * along_y, 4) + lax.rem(x + d * (1 - along_y), 4)

    def span(start, rows):
        return pl.ds(pl.multiple_of(start, 8), rows)

    got = []
    for d in (2, 1, 3):
        to = lax.rem(first + d, 4)
        got.append(go(half_ref.at[span(to * line, line)], rxp.at[d - 1], "feature", partner(0, d)))
    spread_end(0)
    spread(1)

    def project(*steps):
        a, b = [], []
        for step in steps:
            row, col = lax.rem(y + step, 4), lax.rem(x + step, 4)
            a += [yall[0, row].reshape(big, k), yall[1, :, col].reshape(big, k)]
            b += [slab_ref[0, row].reshape(big, -1), slab_ref[1, :, col].reshape(big, -1)]
        a, b = jnp.concatenate(a, axis=0), jnp.concatenate(b, axis=0)
        p = lax.dot_general(a, b, (((0,), (0,)), ((), ())), preferred_element_type=F32)
        zacc[...] = p if steps == (0,) else zacc[...] + p

    project(0)
    for copy in got:
        copy.wait_recv()
    line_ref[...] = half_ref[span(first * line, line), :] + (rxp[0] + rxp[1] + rxp[2])
    got = []
    for d in (2, 1, 3):
        to = lax.rem(second + d, 4)
        got.append(go(line_ref.at[span(to * share_rows, share_rows)], rxq.at[d - 1], "feature", partner(1, d)))
    for copy in got:
        copy.wait_recv()
    rxz[z] = line_ref[span(second * share_rows, share_rows), :] + (rxq[0] + rxq[1] + rxq[2])
    token(nz // 2 - 1)
    got = []
    for d in range(1, nz):
        got.append(go(rxz.at[z], rxz.at[z], "sample", lax.rem(s + 2 * d, 2 * nz)))
    for copy in got:
        copy.wait_recv()
    total = rxz[0]
    for d in range(1, nz):
        total += rxz[d]
    own = span(base + first * line + second * share_rows, share_rows)
    gsum[own, :] = total
    got = []
    for d in (2, 1, 3):
        got.append(go(gsum.at[own], gsum.at[own], "feature", partner(1, d)))
    spread_far(1)
    for copy in got:
        copy.wait_recv()
    own = span(base + first * line, line)
    got = []
    for d in (2, 1, 3):
        got.append(go(gsum.at[own], gsum.at[own], "feature", partner(0, d)))
    project(1, 3)
    for copy in got:
        copy.wait_recv()
    whole = pl.ds(base, mine)
    pair = go(gsum.at[whole], gsum.at[whole], "sample", twin)

    keep = k // 2
    hops = nz // 2

    def columns(pos):
        return pl.ds(pl.multiple_of(pos * B, B), B)

    order = sorted(range(nz), key=lambda d: -min(d, nz - d))
    theirs = {}
    for d in order:
        col = columns(lax.rem(z + d, nz))
        theirs[d] = plan(
            zacc.at[pl.ds(pl.multiple_of((1 - c) * keep, 8), keep), col], rxt.at[:, col], "sample", twin
        )

    def finish_product():
        spread_end(1)
        project(2)
        for d in order:
            theirs[d].start()

    ring = {}
    for way in range(2):
        to = 2 * lax.rem(z + (1 if way == 0 else nz - 1), nz) + c
        for j in range(hops):
            part_rows = pl.ds(0, keep // 2 if j == 0 else keep)
            ring[way, j] = plan(txr.at[way, j, part_rows], rxr.at[way, j, part_rows], "sample", to)
    mid = keep // 2

    def chunk(pos, lo=0, hi=keep):
        col = columns(pos)
        return zacc[pl.ds(pl.multiple_of(c * keep + lo, 8), hi - lo), col] + rxt[lo:hi, col]

    def hop(j):
        for way in range(2):
            d = hops - j if way == 0 else nz - hops + j
            pos = lax.rem(z + d, nz)
            if j or way == 0:
                theirs[d].wait_recv()
            lo = way * mid
            if j == 0:
                txr[way, 0, :mid] = chunk(pos, lo, lo + mid)
            else:
                ring[way, j - 1].wait_recv()
                if j == 1:
                    rest = mid - lo
                    txr[way, 1, lo : lo + mid] = chunk(pos, lo, lo + mid) + rxr[way, 0, :mid]
                    txr[way, 1, rest : rest + mid] = chunk(pos, rest, rest + mid)
                else:
                    txr[way, j] = chunk(pos) + rxr[way, j - 1]
            ring[way, j].start()

    ours = pl.ds(pl.multiple_of(c * keep, 8), keep)
    last = plan(zc.at[ours], zc.at[ours], "sample", twin)

    def meet():
        theirs[0].wait_recv()
        for way in range(2):
            ring[way, hops - 1].wait_recv()
        zc[ours, :] = chunk(z) + (rxr[0, hops - 1] + rxr[1, hops - 1])
        last.start()

    give = []
    for d in range(1, nz):
        to = lax.rem(z + d, nz)
        give.append(plan(cout.at[to], out_ref.at[:, columns(z)], "sample", 2 * to + c))

    def hand_out(lo, hi):
        if lo == 0:
            last.wait_recv()
        part_rows = out_ref.shape[0]
        picked = [inv_ref[pl.ds(pl.multiple_of((2 * j + c) * part_rows, 8), part_rows), :] for j in range(lo, hi)]
        p = high(jnp.concatenate(picked, axis=0), zc[...]) * unit
        cout[lo:hi] = p.reshape(hi - lo, part_rows, B)
        for d in range(1, nz):
            to = lax.rem(z + d, nz)
            pl.when(jnp.logical_and(to >= lo, to < hi))(give[d - 1].start)

    pair.wait_recv()
    n = k
    rid = lax.broadcasted_iota(jnp.int32, (B, B), 0)
    cid = lax.broadcasted_iota(jnp.int32, (B, B), 1)
    top = jnp.zeros((B, B), F32)
    for i in range(nb):
        last_of_row = (i + 1) * (i + 2) // 2 * B
        top = jnp.maximum(top, gsum[last_of_row - B : last_of_row, :])
    top = jnp.max(jnp.where(rid == cid, top, 0.0), axis=(0, 1), keepdims=True)
    unit = lax.rsqrt(top)
    at = 0
    for i in range(nb):
        for j in range(i + 1):
            tile = gsum[at * B : (at + 1) * B, :] * (unit * unit)
            w[i * B : (i + 1) * B, j * B : (j + 1) * B] = tile
            if j < i:
                w[j * B : (j + 1) * B, i * B : (i + 1) * B] = tile.T
            at += 1
    out_scale = (1.0 / math.sqrt(tokens)) / unit
    inv_ref[...] = jnp.zeros_like(inv_ref)
    factor_ref[...] = jnp.zeros_like(factor_ref)

    def finish(i, low):
        at, end = i * B, (i + 1) * B
        span = slice(at, end)
        factor_ref[span, span] = jnp.where(cid >= rid, high(low, w[span, span]), 0.0) * out_scale
        inv_ref[span, span] = low
        if at:
            left = high(low, w[span, :at])
            inv_ref[span, :at] = left
        if end < n:
            right = high(low, w[span, end:])
            factor_ref[span, end:] = right * out_scale
            coef = right.T
            w[end:, end:] -= high(coef, right)
            w[end:, span] = -high(coef, low)
            if at:
                w[end:, :at] -= high(coef, left)

    slots = {
        1: finish_product,
        2: lambda: hop(0),
        4: lambda: hop(1),
        7: lambda: hop(2),
        10: lambda: hop(3),
        13: meet,
        15: lambda: hand_out(0, nz - 2),
    }

    def step(i, _):
        at = pl.multiple_of(i * B, B)

        def hook(quarter):
            for j, work in slots.items():
                if j % 4 == quarter:
                    pl.when(i == j // 4)(work)

        hook(0)
        rows_here = w[pl.ds(at, B), pl.ds(at, B)].reshape(B // 8, 8, B)
        low = inverse_factor(rows_here, row_ref, hook)
        for j in range(nb):
            pl.when(i == j)(functools.partial(finish, j, low))
        return 0

    lax.fori_loop(0, nb, step, 0)

    store = pltpu.make_async_copy(factor_ref, factor_hbm, load_sem.at[len(loads)])
    store.start()

    hand_out(nz - 2, nz)
    out_ref[:, columns(z)] = cout[z]
    for copy in give:
        copy.wait_recv()
    for copy in copies:
        copy.wait_send()
    store.wait()


def hand_over(a_ref, b_ref, a_out, b_out, a_buf, b_buf, sem):
    rows = b_ref.shape[0] // 4
    jobs = [(a_ref, a_buf, a_out)]
    for j in range(4):
        part = pl.ds(j * rows, rows)
        jobs.append((b_ref.at[part], b_buf.at[part], b_out.at[part]))
    copies = [pltpu.make_async_copy(src, buf, sem.at[0, n]) for n, (src, buf, _) in enumerate(jobs)]
    for copy in copies:
        copy.start()
    after = [pltpu.make_async_copy(buf, dst, sem.at[1, n]) for n, (_, buf, dst) in enumerate(jobs)]
    for copy, then in zip(copies, after):
        copy.wait()
        then.start()
    for then in after:
        then.wait()


def shards(slab, omega):
    tokens, width = slab.shape
    depth, k = omega.shape
    nf, ns = lax.axis_size("feature"), lax.axis_size("sample")
    nz = ns // 2
    part = tokens // (2 * nf)
    bit = part // 2
    nb = k // B
    packed = nb * (nb + 1) // 2 * B
    mine = packed // 2
    share = mine // nf
    keep = k // 2
    sems = 48 + 16 + 2 * nf + 2 * nz + 4 * (nz // 2) + nz + 8
    found = pl.pallas_call(
        functools.partial(kernel, 1.0 / math.sqrt(24.0 * D), tokens * ns),
        out_shape=(jax.ShapeDtypeStruct((k // ns, width), F32), jax.ShapeDtypeStruct((k, k), F32)),
        in_specs=[HBM, HBM],
        out_specs=[VMEM, HBM],
        scratch_shapes=[
            pltpu.VMEM((2, 4, 4, part, width), BF16),
            pltpu.VMEM((depth, k), omega.dtype),
            pltpu.VMEM((k, k), F32),
            pltpu.SemaphoreType.DMA((10,)),
            pltpu.VMEM((depth, k), BF16),
            pltpu.VMEM((4, 2, 3, part, k), BF16),
            pltpu.VMEM((4, 2, 3, part, k), BF16),
            pltpu.VMEM((4, 2, part, k), F32),
            pltpu.VMEM((4, 2 * part, k), F32),
            pltpu.VMEM((4, 2, 3, bit // 2, k), F32),
            pltpu.VMEM((4, 2, 3, bit // 2, k), F32),
            pltpu.VMEM((4, bit, k), F32),
            pltpu.VMEM((2, 4, 4, part, k), BF16),
            pltpu.VMEM((packed, B), F32),
            pltpu.VMEM((mine, B), F32),
            pltpu.VMEM((mine, B), F32),
            pltpu.VMEM((3, 4 * share, B), F32),
            pltpu.VMEM((4 * share, B), F32),
            pltpu.VMEM((3, share, B), F32),
            pltpu.VMEM((nz, share, B), F32),
            pltpu.VMEM((packed, B), F32),
            pltpu.VMEM((k, width), F32),
            pltpu.VMEM((keep, width), F32),
            pltpu.VMEM((2, nz // 2, keep, B), F32),
            pltpu.VMEM((2, nz // 2, keep, B), F32),
            pltpu.VMEM((k, B), F32),
            pltpu.VMEM((nz, k // ns, B), F32),
            pltpu.VMEM((k, k), F32),
            pltpu.VMEM((10, 8, B), F32),
            pltpu.VMEM((k, k), F32),
            pltpu.SemaphoreType.DMA((sems,)),
            pltpu.SemaphoreType.DMA((sems,)),
            pltpu.SemaphoreType.REGULAR((nz // 2 - 1,)),
        ],
        compiler_params=pltpu.CompilerParams(collective_id=0, has_side_effects=True, vmem_limit_bytes=56 * MIB),
        name="range_finder",
    )(slab.reshape(2, 4, 4, part, width), omega)
    return pl.pallas_call(
        hand_over,
        out_shape=tuple(jax.ShapeDtypeStruct(a.shape, a.dtype) for a in found),
        in_specs=[HBM, HBM],
        out_specs=[HBM, HBM],
        scratch_shapes=[
            *(pltpu.VMEM(a.shape, a.dtype) for a in found),
            pltpu.SemaphoreType.DMA((2, 5)),
        ],
        compiler_params=pltpu.CompilerParams(vmem_limit_bytes=56 * MIB),
        name="hand_over",
    )(*found)


def solution(mesh):
    placed = (P("sample", "feature"), P("feature", None))
    return jax.shard_map(
        shards, mesh=mesh, in_specs=placed, out_specs=(P("sample", "feature"), P()), check_vma=False
    )
```

```python
import functools
import math

import jax
import jax.numpy as jnp
from jax import lax
from jax.experimental import pallas as pl
from jax.experimental.pallas import tpu as pltpu
from jax.sharding import PartitionSpec as P

D = 16384
F32 = jnp.float32
BF16 = jnp.bfloat16
HIGH = lax.Precision.HIGHEST
MIB = 1 << 20
B = 128
VMEM = pl.BlockSpec(memory_space=pltpu.VMEM)
HBM = pl.BlockSpec(memory_space=pl.ANY)


def remote(src, dst, send_sem, recv_sem, axis, index):
    return pltpu.make_async_remote_copy(
        src_ref=src,
        dst_ref=dst,
        send_sem=send_sem,
        recv_sem=recv_sem,
        device_id={axis: index},
        device_id_type=pl.DeviceIdType.MESH,
    )


def greet(barrier, axis, index):
    pl.semaphore_signal(barrier, inc=1, device_id={axis: index}, device_id_type=pl.DeviceIdType.MESH)


def rep(a):
    return jnp.broadcast_to(a, a.shape[:-2] + (8, 128))


def inverse_factor(s, rows, hook):
    n = s.shape[0]
    sub = lax.broadcasted_iota(jnp.int32, (8, 128), 0)
    lane = lax.broadcasted_iota(jnp.int32, (8, 128), 1)
    s = [s[q] for q in range(n)]
    x = [jnp.where(sub + 8 * q == lane, 1.0, 0.0) for q in range(n)]
    out = []
    for p in range(n):
        if p and p % (n // 4) == 0:
            hook(p // (n // 4))
        cols = [rep(s[p][:, 8 * p + c : 8 * p + c + 1]) for c in range(8)]
        for c in range(8):
            rows[c] = cols[c]
        rows[8] = s[p]
        rows[9] = x[p]
        e = {(r, c): rep(rows[c, r : r + 1]) for c in range(8) for r in range(c, 8)}
        rg = [rep(rows[8, r : r + 1]) for r in range(8)]
        rx = [rep(rows[9, r : r + 1]) for r in range(8)]
        m, wg, wx = {}, [None] * 8, [None] * 8
        for r in range(0, 8, 2):
            a, b, d = e[r, r], e[r + 1, r], e[r + 1, r + 1]
            idet = 1.0 / (a * d - b * b)
            ia = 1.0 / a
            for t in range(r + 2, 8):
                m[t, r] = (e[t, r] * d - e[t, r + 1] * b) * idet
                m[t, r + 1] = (e[t, r + 1] * a - e[t, r] * b) * idet
            for t in range(r + 2, 8):
                for c in range(r + 2, t + 1):
                    e[t, c] = e[t, c] - (m[t, r] * e[c, r] + m[t, r + 1] * e[c, r + 1])
            for t in range(r + 2, 8):
                rg[t] = rg[t] - (m[t, r] * rg[r] + m[t, r + 1] * rg[r + 1])
                rx[t] = rx[t] - (m[t, r] * rx[r] + m[t, r + 1] * rx[r + 1])
            for v, w in ((rg, wg), (rx, wx)):
                w[r] = (v[r] * d - v[r + 1] * b) * idet
                w[r + 1] = (v[r + 1] * a - v[r] * b) * idet
            o0 = rx[r] * lax.rsqrt(a)
            o1 = (rx[r + 1] - (b * ia) * rx[r]) * lax.rsqrt((a * d - b * b) * ia)
            ox = o0 if r == 0 else jnp.where(sub == r, o0, ox)
            ox = jnp.where(sub == r + 1, o1, ox)
        out.append(ox)
        if p + 1 < n:
            for r in range(6, 0, -2):
                for t in range(r):
                    wg[t] = wg[t] - (m[r, t] * wg[r] + m[r + 1, t] * wg[r + 1])
                    wx[t] = wx[t] - (m[r, t] * wx[r] + m[r + 1, t] * wx[r + 1])
            for q in range(p + 1, n):
                k = [rep(s[q][:, 8 * p + c : 8 * p + c + 1]) for c in range(8)]
                for w, v in ((wg, s), (wx, x)):
                    t = [k[c] * w[c] for c in range(8)]
                    v[q] = v[q] - (((t[0] + t[1]) + (t[2] + t[3])) + ((t[4] + t[5]) + (t[6] + t[7])))
    return jnp.concatenate(out, axis=0)


def high(a, b):
    return jnp.dot(a, b, precision=HIGH, preferred_element_type=F32)


def kernel(
    scale, tokens, slab_hbm, omega_hbm, out_ref, factor_hbm,
    slab_ref, omega_ref, factor_ref, load_sem, wide, tx1, rx1, side1, own1, tx2, rx2, sum2,
    yall, packed, rx0, half_ref, rxp, rxz, gsum,
    zacc, rxt, txr, rxr, zc, cout, w, row_ref, inv_ref, send_sem, recv_sem,
):
    f, s = lax.axis_index("feature"), lax.axis_index("sample")
    nf, nz = lax.axis_size("feature"), lax.axis_size("sample") // 2
    x, y = lax.rem(f, 4), f // 4
    z, c = s // 2, lax.rem(s, 2)
    twin = 2 * z + 1 - c
    barrier = pltpu.get_barrier_semaphore()
    greet(barrier, "sample", twin)
    for d in range(1, nf):
        greet(barrier, "feature", lax.rem(f + d, nf))
    for d in range(1, nz):
        greet(barrier, "sample", lax.rem(s + 2 * d, 2 * nz))

    loads = {}
    here = (lax.rem(f, 4), f // 4)

    def load(n, src, dst):
        loads[n] = pltpu.make_async_copy(src, dst, load_sem.at[len(loads)])
        loads[n].start()

    def tokens_of(ref, half, pos):
        return ref.at[half, :, pos] if half == 0 else ref.at[half, pos]

    load("omega", omega_hbm, omega_ref)
    for step in (2, 1, 3, 0):
        for half in range(2):
            pos = lax.rem(here[half] + step, 4)
            load((half, step), tokens_of(slab_hbm, half, pos), tokens_of(slab_ref, half, pos))
    ready = set()

    copies = []
    count = [0]

    def plan(src, dst, axis, to):
        n = count[0]
        count[0] += 1
        copy = remote(src, dst, send_sem.at[n], recv_sem.at[n], axis, to)
        copies.append(copy)
        return copy

    def go(src, dst, axis, to):
        copy = plan(src, dst, axis, to)
        copy.start()
        return copy

    def node(axis, pos):
        return 4 * y + pos if axis == 0 else 4 * pos + x

    def beside(axis, way):
        return node(axis, lax.rem(here[axis] + (1 if way == 0 else 3), 4))

    loads["omega"].wait()
    wide[...] = omega_ref[...].astype(BF16)
    part = yall.shape[3]
    k = yall.shape[4]
    big = 4 * part
    small = part // 2
    bit = part // 2
    cut = 2 * bit
    fine = bit // 2
    units = [(half, batch) for batch in range(2) for half in range(2)]

    def product(half, batch, step):
        if (half, step) not in ready:
            ready.add((half, step))
            loads[half, step].wait()
        pos = lax.rem(here[half] + step, 4)
        lines = pl.ds(batch * bit, bit)
        a = slab_ref[0, :, pos, lines] if half == 0 else slab_ref[1, pos, :, lines]
        return jnp.dot(a.reshape(4 * bit, -1), wide[...], preferred_element_type=F32)

    sent = {}

    def pass_on(stage, u, way, piece):
        half = units[u][0]
        axis = half if stage == 0 else 1 - half
        tx, rx = (tx1, rx1) if stage == 0 else (tx2, rx2)
        sent[stage, u, way, piece] = go(tx.at[u, way, piece], rx.at[u, way, piece], "feature", beside(axis, way))

    for batch in range(2):
        now = (2 * batch, 2 * batch + 1)
        for u in now:
            far = product(*units[u], 2).astype(BF16)
            tx1[u, 0, 0] = far[:cut]
            tx1[u, 1, 0] = far[cut:]
            if u == 0:
                pl.semaphore_wait(barrier, nf + nz - 1)
            pass_on(0, u, 0, 0)
            pass_on(0, u, 1, 0)
        for u in now:
            right = product(*units[u], 1)
            tx1[u, 0, 1] = right[cut:].astype(BF16)
            pass_on(0, u, 0, 1)
            side1[u, 0] = right[:cut]
            left = product(*units[u], 3)
            tx1[u, 1, 1] = left[:cut].astype(BF16)
            pass_on(0, u, 1, 1)
            side1[u, 1] = left[cut:]
        for u in now:
            for way in range(2):
                sent[0, u, way, 0].wait_recv()
                tx1[u, way, 2] = (side1[u, way] + rx1[u, way, 0].astype(F32)).astype(BF16)
                pass_on(0, u, way, 2)
    for u in range(4):
        own1[u] = product(*units[u], 0)
    for u in range(4):
        half = units[u][0]
        for way in range(2):
            sent[0, u, way, 1].wait_recv()
        own1[u, cut:] += rx1[u, 0, 1].astype(F32)
        own1[u, :cut] += rx1[u, 1, 1].astype(F32)
        for way in range(2):
            sent[0, u, way, 2].wait_recv()
        own1[u, :cut] += rx1[u, 0, 2].astype(F32)
        own1[u, cut:] += rx1[u, 1, 2].astype(F32)

        def block(pos, lo, hi):
            return own1[u, pl.ds(pl.multiple_of(pos * bit + lo, 8), hi - lo), :]

        pos = here[1 - half]
        far, right, left = (lax.rem(pos + step, 4) for step in (2, 1, 3))
        tx2[u, 0, 0] = block(far, 0, fine)
        pass_on(1, u, 0, 0)
        tx2[u, 1, 0] = block(far, fine, bit)
        pass_on(1, u, 1, 0)
        tx2[u, 0, 1] = block(right, fine, bit)
        pass_on(1, u, 0, 1)
        tx2[u, 1, 1] = block(left, 0, fine)
        pass_on(1, u, 1, 1)
        tx2[u, 0, 2] = block(right, 0, fine)
        tx2[u, 1, 2] = block(left, fine, bit)
        sum2[u] = block(pos, 0, bit)
    for u in range(4):
        for way in range(2):
            sent[1, u, way, 0].wait_recv()
            tx2[u, way, 2] += rx2[u, way, 0]
            pass_on(1, u, way, 2)
    for u in range(4):
        half, batch = units[u]
        for way in range(2):
            sent[1, u, way, 1].wait_recv()
            sent[1, u, way, 2].wait_recv()
        lower = (sum2[u, fine:] + (rx2[u, 0, 1] + rx2[u, 1, 2])) * scale
        upper = (sum2[u, :fine] + (rx2[u, 1, 1] + rx2[u, 0, 2])) * scale
        yall[half, y, x, batch * bit : (batch + 1) * bit] = jnp.concatenate([upper, lower], axis=0).astype(BF16)
    mine_y = [yall[half, y, x] for half in range(2)]

    def held(half, stage, px, py, lo=None):
        if stage == 0:
            ref = yall.at[half, py, px]
            return ref if lo is None else ref.at[pl.ds(lo * small, small)]
        if half == 0:
            ref = yall.at[half, py]
            return ref if lo is None else ref.at[pl.ds(2 * lo, 2)]
        return yall.at[half, :, px] if lo is None else yall.at[half, pl.ds(2 * lo, 2), px]

    near, relay = {}, {}

    def spread(stage):
        for half in range(2):
            axis = half if stage == 0 else 1 - half
            for way in range(2):
                ref = held(half, stage, x, y)
                near[stage, half, way] = go(ref, ref, "feature", beside(axis, way))

    def spread_far(stage):
        for half in range(2):
            axis = half if stage == 0 else 1 - half
            for way in range(2):
                near[stage, half, way].wait_recv()
                back = lax.rem(here[axis] + (3 if way == 0 else 1), 4)
                px, py = (back, y) if axis == 0 else (x, back)
                ref = held(half, stage, px, py, way)
                relay[stage, half, way] = go(ref, ref, "feature", beside(axis, way))

    def spread_end(stage):
        for half in range(2):
            for way in range(2):
                relay[stage, half, way].wait_recv()

    spread(0)

    ys = jnp.concatenate(mine_y, axis=0)
    yt = ys.T
    nb = k // B
    at = 0
    for i in range(nb):
        row = jnp.dot(yt[i * B : (i + 1) * B], ys[:, : (i + 1) * B], preferred_element_type=F32)
        for j in range(i + 1):
            packed[at * B : (at + 1) * B, :] = row[:, j * B : (j + 1) * B]
            at += 1
    mine = at * B // 2
    share_rows = mine // nf
    base = pl.multiple_of(c * mine, 8)
    other = pl.multiple_of((1 - c) * mine, 8)
    pair = go(packed.at[pl.ds(other, mine)], rx0, "sample", twin)
    spread_far(0)
    pair.wait_recv()
    half_ref[...] = packed[pl.ds(base, mine), :] + rx0[...]

    def share(p):
        return pl.ds(pl.multiple_of(p * share_rows, 8), share_rows)

    got = []
    for d in range(1, nf):
        to = lax.rem(f + d, nf)
        got.append(go(half_ref.at[share(to)], rxp.at[d - 1], "feature", to))
    spread_end(0)
    spread(1)

    def project(*steps):
        a, b = [], []
        for step in steps:
            row, col = lax.rem(y + step, 4), lax.rem(x + step, 4)
            a += [yall[0, row].reshape(big, k), yall[1, :, col].reshape(big, k)]
            b += [slab_ref[0, row].reshape(big, -1), slab_ref[1, :, col].reshape(big, -1)]
        a, b = jnp.concatenate(a, axis=0), jnp.concatenate(b, axis=0)
        p = lax.dot_general(a, b, (((0,), (0,)), ((), ())), preferred_element_type=F32)
        zacc[...] = p if steps == (0,) else zacc[...] + p

    project(0)
    for copy in got:
        copy.wait_recv()
    total = half_ref[share(f), :]
    for d in range(1, nf):
        total += rxp[d - 1]
    rxz[z] = total
    got = []
    for d in range(1, nz):
        got.append(go(rxz.at[z], rxz.at[z], "sample", lax.rem(s + 2 * d, 2 * nz)))
    for copy in got:
        copy.wait_recv()
    total = rxz[0]
    for d in range(1, nz):
        total += rxz[d]
    own = pl.ds(pl.multiple_of(base + f * share_rows, 8), share_rows)
    gsum[own, :] = total
    got = []
    for d in range(1, nf):
        got.append(go(gsum.at[own], gsum.at[own], "feature", lax.rem(f + d, nf)))
    spread_far(1)
    project(1, 3)
    for copy in got:
        copy.wait_recv()
    whole = pl.ds(base, mine)
    pair = go(gsum.at[whole], gsum.at[whole], "sample", twin)

    keep = k // 2
    hops = nz // 2

    def columns(pos):
        return pl.ds(pl.multiple_of(pos * B, B), B)

    order = sorted(range(nz), key=lambda d: -min(d, nz - d))
    theirs = {}
    for d in order:
        col = columns(lax.rem(z + d, nz))
        theirs[d] = plan(
            zacc.at[pl.ds(pl.multiple_of((1 - c) * keep, 8), keep), col], rxt.at[:, col], "sample", twin
        )

    def finish_product():
        spread_end(1)
        project(2)
        for d in order:
            theirs[d].start()

    ring = {}
    for way in range(2):
        to = 2 * lax.rem(z + (1 if way == 0 else nz - 1), nz) + c
        for j in range(hops):
            part_rows = pl.ds(0, keep // 2 if j == 0 else keep)
            ring[way, j] = plan(txr.at[way, j, part_rows], rxr.at[way, j, part_rows], "sample", to)
    mid = keep // 2

    def chunk(pos, lo=0, hi=keep):
        col = columns(pos)
        return zacc[pl.ds(pl.multiple_of(c * keep + lo, 8), hi - lo), col] + rxt[lo:hi, col]

    def hop(j):
        for way in range(2):
            d = hops - j if way == 0 else nz - hops + j
            pos = lax.rem(z + d, nz)
            if j or way == 0:
                theirs[d].wait_recv()
            lo = way * mid
            if j == 0:
                txr[way, 0, :mid] = chunk(pos, lo, lo + mid)
            else:
                ring[way, j - 1].wait_recv()
                if j == 1:
                    rest = mid - lo
                    txr[way, 1, lo : lo + mid] = chunk(pos, lo, lo + mid) + rxr[way, 0, :mid]
                    txr[way, 1, rest : rest + mid] = chunk(pos, rest, rest + mid)
                else:
                    txr[way, j] = chunk(pos) + rxr[way, j - 1]
            ring[way, j].start()

    ours = pl.ds(pl.multiple_of(c * keep, 8), keep)
    last = plan(zc.at[ours], zc.at[ours], "sample", twin)

    def meet():
        theirs[0].wait_recv()
        for way in range(2):
            ring[way, hops - 1].wait_recv()
        zc[ours, :] = chunk(z) + (rxr[0, hops - 1] + rxr[1, hops - 1])
        last.start()

    give = []
    for d in range(1, nz):
        to = lax.rem(z + d, nz)
        give.append(plan(cout.at[to], out_ref.at[:, columns(z)], "sample", 2 * to + c))

    def hand_out(lo, hi):
        if lo == 0:
            last.wait_recv()
        part_rows = out_ref.shape[0]
        picked = [inv_ref[pl.ds(pl.multiple_of((2 * j + c) * part_rows, 8), part_rows), :] for j in range(lo, hi)]
        p = high(jnp.concatenate(picked, axis=0), zc[...]) * unit
        cout[lo:hi] = p.reshape(hi - lo, part_rows, B)
        for d in range(1, nz):
            to = lax.rem(z + d, nz)
            pl.when(jnp.logical_and(to >= lo, to < hi))(give[d - 1].start)

    pair.wait_recv()
    n = k
    rid = lax.broadcasted_iota(jnp.int32, (B, B), 0)
    cid = lax.broadcasted_iota(jnp.int32, (B, B), 1)
    top = jnp.zeros((B, B), F32)
    for i in range(nb):
        last_of_row = (i + 1) * (i + 2) // 2 * B
        top = jnp.maximum(top, gsum[last_of_row - B : last_of_row, :])
    top = jnp.max(jnp.where(rid == cid, top, 0.0), axis=(0, 1), keepdims=True)
    unit = lax.rsqrt(top)
    at = 0
    for i in range(nb):
        for j in range(i + 1):
            tile = gsum[at * B : (at + 1) * B, :] * (unit * unit)
            w[i * B : (i + 1) * B, j * B : (j + 1) * B] = tile
            if j < i:
                w[j * B : (j + 1) * B, i * B : (i + 1) * B] = tile.T
            at += 1
    out_scale = (1.0 / math.sqrt(tokens)) / unit
    inv_ref[...] = jnp.zeros_like(inv_ref)
    factor_ref[...] = jnp.zeros_like(factor_ref)

    def finish(i, low):
        at, end = i * B, (i + 1) * B
        span = slice(at, end)
        factor_ref[span, span] = jnp.where(cid >= rid, high(low, w[span, span]), 0.0) * out_scale
        inv_ref[span, span] = low
        if at:
            left = high(low, w[span, :at])
            inv_ref[span, :at] = left
        if end < n:
            right = high(low, w[span, end:])
            factor_ref[span, end:] = right * out_scale
            coef = right.T
            w[end:, end:] -= high(coef, right)
            w[end:, span] = -high(coef, low)
            if at:
                w[end:, :at] -= high(coef, left)

    slots = {
        1: finish_product,
        2: lambda: hop(0),
        4: lambda: hop(1),
        7: lambda: hop(2),
        10: lambda: hop(3),
        13: meet,
        15: lambda: hand_out(0, nz - 2),
    }

    def step(i, _):
        at = pl.multiple_of(i * B, B)

        def hook(quarter):
            for j, work in slots.items():
                if j % 4 == quarter:
                    pl.when(i == j // 4)(work)

        hook(0)
        rows_here = w[pl.ds(at, B), pl.ds(at, B)].reshape(B // 8, 8, B)
        low = inverse_factor(rows_here, row_ref, hook)
        for j in range(nb):
            pl.when(i == j)(functools.partial(finish, j, low))
        return 0

    lax.fori_loop(0, nb, step, 0)

    store = pltpu.make_async_copy(factor_ref, factor_hbm, load_sem.at[len(loads)])
    store.start()

    hand_out(nz - 2, nz)
    out_ref[:, columns(z)] = cout[z]
    for copy in give:
        copy.wait_recv()
    for copy in copies:
        copy.wait_send()
    store.wait()


def hand_over(a_ref, b_ref, a_out, b_out, a_buf, b_buf, sem):
    rows = b_ref.shape[0] // 4
    jobs = [(a_ref, a_buf, a_out)]
    for j in range(4):
        part = pl.ds(j * rows, rows)
        jobs.append((b_ref.at[part], b_buf.at[part], b_out.at[part]))
    copies = [pltpu.make_async_copy(src, buf, sem.at[0, n]) for n, (src, buf, _) in enumerate(jobs)]
    for copy in copies:
        copy.start()
    after = [pltpu.make_async_copy(buf, dst, sem.at[1, n]) for n, (_, buf, dst) in enumerate(jobs)]
    for copy, then in zip(copies, after):
        copy.wait()
        then.start()
    for then in after:
        then.wait()


def shards(slab, omega):
    tokens, width = slab.shape
    depth, k = omega.shape
    nf, ns = lax.axis_size("feature"), lax.axis_size("sample")
    nz = ns // 2
    part = tokens // (2 * nf)
    bit = part // 2
    nb = k // B
    packed = nb * (nb + 1) // 2 * B
    mine = packed // 2
    share = mine // nf
    keep = k // 2
    sems = 48 + 16 + 2 * nf + 2 * nz + 4 * (nz // 2) + nz + 8
    found = pl.pallas_call(
        functools.partial(kernel, 1.0 / math.sqrt(24.0 * D), tokens * ns),
        out_shape=(jax.ShapeDtypeStruct((k // ns, width), F32), jax.ShapeDtypeStruct((k, k), F32)),
        in_specs=[HBM, HBM],
        out_specs=[VMEM, HBM],
        scratch_shapes=[
            pltpu.VMEM((2, 4, 4, part, width), BF16),
            pltpu.VMEM((depth, k), omega.dtype),
            pltpu.VMEM((k, k), F32),
            pltpu.SemaphoreType.DMA((10,)),
            pltpu.VMEM((depth, k), BF16),
            pltpu.VMEM((4, 2, 3, part, k), BF16),
            pltpu.VMEM((4, 2, 3, part, k), BF16),
            pltpu.VMEM((4, 2, part, k), F32),
            pltpu.VMEM((4, 2 * part, k), F32),
            pltpu.VMEM((4, 2, 3, bit // 2, k), F32),
            pltpu.VMEM((4, 2, 3, bit // 2, k), F32),
            pltpu.VMEM((4, bit, k), F32),
            pltpu.VMEM((2, 4, 4, part, k), BF16),
            pltpu.VMEM((packed, B), F32),
            pltpu.VMEM((mine, B), F32),
            pltpu.VMEM((mine, B), F32),
            pltpu.VMEM((nf - 1, share, B), F32),
            pltpu.VMEM((nz, share, B), F32),
            pltpu.VMEM((packed, B), F32),
            pltpu.VMEM((k, width), F32),
            pltpu.VMEM((keep, width), F32),
            pltpu.VMEM((2, nz // 2, keep, B), F32),
            pltpu.VMEM((2, nz // 2, keep, B), F32),
            pltpu.VMEM((k, B), F32),
            pltpu.VMEM((nz, k // ns, B), F32),
            pltpu.VMEM((k, k), F32),
            pltpu.VMEM((10, 8, B), F32),
            pltpu.VMEM((k, k), F32),
            pltpu.SemaphoreType.DMA((sems,)),
            pltpu.SemaphoreType.DMA((sems,)),
        ],
        compiler_params=pltpu.CompilerParams(collective_id=0, has_side_effects=True, vmem_limit_bytes=56 * MIB),
        name="range_finder",
    )(slab.reshape(2, 4, 4, part, width), omega)
    return pl.pallas_call(
        hand_over,
        out_shape=tuple(jax.ShapeDtypeStruct(a.shape, a.dtype) for a in found),
        in_specs=[HBM, HBM],
        out_specs=[HBM, HBM],
        scratch_shapes=[
            *(pltpu.VMEM(a.shape, a.dtype) for a in found),
            pltpu.SemaphoreType.DMA((2, 5)),
        ],
        compiler_params=pltpu.CompilerParams(vmem_limit_bytes=56 * MIB),
        name="hand_over",
    )(*found)


def solution(mesh):
    placed = (P("sample", "feature"), P("feature", None))
    return jax.shard_map(
        shards, mesh=mesh, in_specs=placed, out_specs=(P("sample", "feature"), P()), check_vma=False
    )
```

```python
import functools
import math

import jax
import jax.numpy as jnp
from jax import lax
from jax.experimental import pallas as pl
from jax.experimental.pallas import tpu as pltpu
from jax.sharding import PartitionSpec as P

D = 16384
F32 = jnp.float32
BF16 = jnp.bfloat16
HIGH = lax.Precision.HIGHEST
MIB = 1 << 20
B = 128
VMEM = pl.BlockSpec(memory_space=pltpu.VMEM)
HBM = pl.BlockSpec(memory_space=pl.ANY)


def remote(src, dst, send_sem, recv_sem, axis, index):
    return pltpu.make_async_remote_copy(
        src_ref=src,
        dst_ref=dst,
        send_sem=send_sem,
        recv_sem=recv_sem,
        device_id={axis: index},
        device_id_type=pl.DeviceIdType.MESH,
    )


def greet(barrier, axis, index):
    pl.semaphore_signal(barrier, inc=1, device_id={axis: index}, device_id_type=pl.DeviceIdType.MESH)


def rep(a):
    return jnp.broadcast_to(a, a.shape[:-2] + (8, 128))


def inverse_factor(s, rows, hook):
    n = s.shape[0]
    sub = lax.broadcasted_iota(jnp.int32, (8, 128), 0)
    lane = lax.broadcasted_iota(jnp.int32, (8, 128), 1)
    s = [s[q] for q in range(n)]
    x = [jnp.where(sub + 8 * q == lane, 1.0, 0.0) for q in range(n)]
    out = []
    for p in range(n):
        if p and p % (n // 4) == 0:
            hook(p // (n // 4))
        cols = [rep(s[p][:, 8 * p + c : 8 * p + c + 1]) for c in range(8)]
        for c in range(8):
            rows[c] = cols[c]
        rows[8] = s[p]
        rows[9] = x[p]
        e = {(r, c): rep(rows[c, r : r + 1]) for c in range(8) for r in range(c, 8)}
        rg = [rep(rows[8, r : r + 1]) for r in range(8)]
        rx = [rep(rows[9, r : r + 1]) for r in range(8)]
        m, wg, wx = {}, [None] * 8, [None] * 8
        for r in range(0, 8, 2):
            a, b, d = e[r, r], e[r + 1, r], e[r + 1, r + 1]
            idet = 1.0 / (a * d - b * b)
            ia = 1.0 / a
            for t in range(r + 2, 8):
                m[t, r] = (e[t, r] * d - e[t, r + 1] * b) * idet
                m[t, r + 1] = (e[t, r + 1] * a - e[t, r] * b) * idet
            for t in range(r + 2, 8):
                for c in range(r + 2, t + 1):
                    e[t, c] = e[t, c] - (m[t, r] * e[c, r] + m[t, r + 1] * e[c, r + 1])
            for t in range(r + 2, 8):
                rg[t] = rg[t] - (m[t, r] * rg[r] + m[t, r + 1] * rg[r + 1])
                rx[t] = rx[t] - (m[t, r] * rx[r] + m[t, r + 1] * rx[r + 1])
            for v, w in ((rg, wg), (rx, wx)):
                w[r] = (v[r] * d - v[r + 1] * b) * idet
                w[r + 1] = (v[r + 1] * a - v[r] * b) * idet
            o0 = rx[r] * lax.rsqrt(a)
            o1 = (rx[r + 1] - (b * ia) * rx[r]) * lax.rsqrt((a * d - b * b) * ia)
            ox = o0 if r == 0 else jnp.where(sub == r, o0, ox)
            ox = jnp.where(sub == r + 1, o1, ox)
        out.append(ox)
        if p + 1 < n:
            for r in range(6, 0, -2):
                for t in range(r):
                    wg[t] = wg[t] - (m[r, t] * wg[r] + m[r + 1, t] * wg[r + 1])
                    wx[t] = wx[t] - (m[r, t] * wx[r] + m[r + 1, t] * wx[r + 1])
            for q in range(p + 1, n):
                k = [rep(s[q][:, 8 * p + c : 8 * p + c + 1]) for c in range(8)]
                for w, v in ((wg, s), (wx, x)):
                    t = [k[c] * w[c] for c in range(8)]
                    v[q] = v[q] - (((t[0] + t[1]) + (t[2] + t[3])) + ((t[4] + t[5]) + (t[6] + t[7])))
    return jnp.concatenate(out, axis=0)


def high(a, b):
    return jnp.dot(a, b, precision=HIGH, preferred_element_type=F32)


def kernel(
    scale, tokens, slab_hbm, omega_hbm, out_ref, factor_hbm,
    slab_ref, omega_ref, factor_ref, load_sem, wide, tx1, rx1, side1, own1, tx2, rx2, sum2,
    yall, packed, rx0, half_ref, rxp, rxz, gsum,
    zacc, rxt, txr, rxr, zc, cout, w, row_ref, inv_ref, send_sem, recv_sem,
):
    f, s = lax.axis_index("feature"), lax.axis_index("sample")
    nf, nz = lax.axis_size("feature"), lax.axis_size("sample") // 2
    x, y = lax.rem(f, 4), f // 4
    z, c = s // 2, lax.rem(s, 2)
    twin = 2 * z + 1 - c
    barrier = pltpu.get_barrier_semaphore()
    greet(barrier, "sample", twin)
    for d in range(1, nf):
        greet(barrier, "feature", lax.rem(f + d, nf))
    for d in range(1, nz):
        greet(barrier, "sample", lax.rem(s + 2 * d, 2 * nz))

    loads = {}
    here = (lax.rem(f, 4), f // 4)

    def load(n, src, dst):
        loads[n] = pltpu.make_async_copy(src, dst, load_sem.at[len(loads)])
        loads[n].start()

    def tokens_of(ref, half, pos):
        return ref.at[half, :, pos] if half == 0 else ref.at[half, pos]

    def load_slab(step):
        for half in range(2):
            pos = lax.rem(here[half] + step, 4)
            load((half, step), tokens_of(slab_hbm, half, pos), tokens_of(slab_ref, half, pos))

    load("omega", omega_hbm, omega_ref)
    load_slab(2)
    ready = set()

    copies = []
    count = [0]

    def plan(src, dst, axis, to):
        n = count[0]
        count[0] += 1
        copy = remote(src, dst, send_sem.at[n], recv_sem.at[n], axis, to)
        copies.append(copy)
        return copy

    def go(src, dst, axis, to):
        copy = plan(src, dst, axis, to)
        copy.start()
        return copy

    def node(axis, pos):
        return 4 * y + pos if axis == 0 else 4 * pos + x

    def beside(axis, way):
        return node(axis, lax.rem(here[axis] + (1 if way == 0 else 3), 4))

    loads["omega"].wait()
    for step in (1, 3, 0):
        load_slab(step)
    wide[...] = omega_ref[...].astype(BF16)
    part = yall.shape[3]
    k = yall.shape[4]
    big = 4 * part
    small = part // 2
    bit = part // 2
    cut = 2 * bit
    fine = bit // 2
    units = [(half, batch) for batch in range(2) for half in range(2)]

    def product(half, batch, step):
        if (half, step) not in ready:
            ready.add((half, step))
            loads[half, step].wait()
        pos = lax.rem(here[half] + step, 4)
        lines = pl.ds(batch * bit, bit)
        a = slab_ref[0, :, pos, lines] if half == 0 else slab_ref[1, pos, :, lines]
        return jnp.dot(a.reshape(4 * bit, -1), wide[...], preferred_element_type=F32)

    sent = {}

    def pass_on(stage, u, way, piece):
        half = units[u][0]
        axis = half if stage == 0 else 1 - half
        tx, rx = (tx1, rx1) if stage == 0 else (tx2, rx2)
        sent[stage, u, way, piece] = go(tx.at[u, way, piece], rx.at[u, way, piece], "feature", beside(axis, way))

    for batch in range(2):
        now = (2 * batch, 2 * batch + 1)
        for u in now:
            far = product(*units[u], 2).astype(BF16)
            tx1[u, 0, 0] = far[:cut]
            tx1[u, 1, 0] = far[cut:]
            if u == 0:
                pl.semaphore_wait(barrier, nf + nz - 1)
            pass_on(0, u, 0, 0)
            pass_on(0, u, 1, 0)
        for u in now:
            right = product(*units[u], 1)
            tx1[u, 0, 1] = right[cut:].astype(BF16)
            pass_on(0, u, 0, 1)
            side1[u, 0] = right[:cut]
            left = product(*units[u], 3)
            tx1[u, 1, 1] = left[:cut].astype(BF16)
            pass_on(0, u, 1, 1)
            side1[u, 1] = left[cut:]
        for u in now:
            for way in range(2):
                sent[0, u, way, 0].wait_recv()
                tx1[u, way, 2] = (side1[u, way] + rx1[u, way, 0].astype(F32)).astype(BF16)
                pass_on(0, u, way, 2)
    for u in range(4):
        own1[u] = product(*units[u], 0)
    for u in range(4):
        half = units[u][0]
        for way in range(2):
            sent[0, u, way, 1].wait_recv()
        own1[u, cut:] += rx1[u, 0, 1].astype(F32)
        own1[u, :cut] += rx1[u, 1, 1].astype(F32)
        for way in range(2):
            sent[0, u, way, 2].wait_recv()
        own1[u, :cut] += rx1[u, 0, 2].astype(F32)
        own1[u, cut:] += rx1[u, 1, 2].astype(F32)

        def block(pos, lo, hi):
            return own1[u, pl.ds(pl.multiple_of(pos * bit + lo, 8), hi - lo), :]

        pos = here[1 - half]
        far, right, left = (lax.rem(pos + step, 4) for step in (2, 1, 3))
        tx2[u, 0, 0] = block(far, 0, fine)
        pass_on(1, u, 0, 0)
        tx2[u, 1, 0] = block(far, fine, bit)
        pass_on(1, u, 1, 0)
        tx2[u, 0, 1] = block(right, fine, bit)
        pass_on(1, u, 0, 1)
        tx2[u, 1, 1] = block(left, 0, fine)
        pass_on(1, u, 1, 1)
        tx2[u, 0, 2] = block(right, 0, fine)
        tx2[u, 1, 2] = block(left, fine, bit)
        sum2[u] = block(pos, 0, bit)
    for u in range(4):
        for way in range(2):
            sent[1, u, way, 0].wait_recv()
            tx2[u, way, 2] += rx2[u, way, 0]
            pass_on(1, u, way, 2)
    for u in range(4):
        half, batch = units[u]
        for way in range(2):
            sent[1, u, way, 1].wait_recv()
            sent[1, u, way, 2].wait_recv()
        lower = (sum2[u, fine:] + (rx2[u, 0, 1] + rx2[u, 1, 2])) * scale
        upper = (sum2[u, :fine] + (rx2[u, 1, 1] + rx2[u, 0, 2])) * scale
        yall[half, y, x, batch * bit : (batch + 1) * bit] = jnp.concatenate([upper, lower], axis=0).astype(BF16)
    mine_y = [yall[half, y, x] for half in range(2)]

    def held(half, stage, px, py, lo=None):
        if stage == 0:
            ref = yall.at[half, py, px]
            return ref if lo is None else ref.at[pl.ds(lo * small, small)]
        if half == 0:
            ref = yall.at[half, py]
            return ref if lo is None else ref.at[pl.ds(2 * lo, 2)]
        return yall.at[half, :, px] if lo is None else yall.at[half, pl.ds(2 * lo, 2), px]

    near, relay = {}, {}

    def spread(stage):
        for lo in range(2):
            for half in range(2):
                axis = half if stage == 0 else 1 - half
                for way in range(2):
                    ref = held(half, stage, x, y, way if lo == 0 else 1 - way)
                    near[stage, half, way, lo] = go(ref, ref, "feature", beside(axis, way))

    def spread_far(stage):
        for half in range(2):
            axis = half if stage == 0 else 1 - half
            for way in range(2):
                near[stage, half, way, 0].wait_recv()
                back = lax.rem(here[axis] + (3 if way == 0 else 1), 4)
                px, py = (back, y) if axis == 0 else (x, back)
                ref = held(half, stage, px, py, way)
                relay[stage, half, way] = go(ref, ref, "feature", beside(axis, way))

    def spread_near(stage):
        for half in range(2):
            for way in range(2):
                near[stage, half, way, 1].wait_recv()

    def spread_end(stage):
        for half in range(2):
            for way in range(2):
                relay[stage, half, way].wait_recv()

    spread(0)

    ys = jnp.concatenate(mine_y, axis=0)
    yt = ys.T
    nb = k // B
    at = 0
    for i in range(nb):
        row = jnp.dot(yt[i * B : (i + 1) * B], ys[:, : (i + 1) * B], preferred_element_type=F32)
        for j in range(i + 1):
            packed[at * B : (at + 1) * B, :] = row[:, j * B : (j + 1) * B]
            at += 1
    mine = at * B // 2
    share_rows = mine // nf
    base = pl.multiple_of(c * mine, 8)
    other = pl.multiple_of((1 - c) * mine, 8)
    pair = go(packed.at[pl.ds(other, mine)], rx0, "sample", twin)
    spread_far(0)
    pair.wait_recv()
    half_ref[...] = packed[pl.ds(base, mine), :] + rx0[...]

    def share(p):
        return pl.ds(pl.multiple_of(p * share_rows, 8), share_rows)

    got = []
    for d in range(1, nf):
        to = lax.rem(f + d, nf)
        got.append(go(half_ref.at[share(to)], rxp.at[d - 1], "feature", to))
    spread_near(0)
    spread_end(0)
    spread(1)

    def project(*steps):
        a, b = [], []
        for step in steps:
            row, col = lax.rem(y + step, 4), lax.rem(x + step, 4)
            a += [yall[0, row].reshape(big, k), yall[1, :, col].reshape(big, k)]
            b += [slab_ref[0, row].reshape(big, -1), slab_ref[1, :, col].reshape(big, -1)]
        a, b = jnp.concatenate(a, axis=0), jnp.concatenate(b, axis=0)
        p = lax.dot_general(a, b, (((0,), (0,)), ((), ())), preferred_element_type=F32)
        zacc[...] = p if steps == (0,) else zacc[...] + p

    project(0)
    for copy in got:
        copy.wait_recv()
    total = half_ref[share(f), :]
    for d in range(1, nf):
        total += rxp[d - 1]
    rxz[z] = total
    got = []
    for d in range(1, nz):
        got.append(go(rxz.at[z], rxz.at[z], "sample", lax.rem(s + 2 * d, 2 * nz)))
    spread_far(1)
    for copy in got:
        copy.wait_recv()
    total = rxz[0]
    for d in range(1, nz):
        total += rxz[d]
    own = pl.ds(pl.multiple_of(base + f * share_rows, 8), share_rows)
    gsum[own, :] = total
    got = []
    for d in range(1, nf):
        got.append(go(gsum.at[own], gsum.at[own], "feature", lax.rem(f + d, nf)))
    spread_near(1)
    project(1, 3)

    keep = k // 2
    hops = nz // 2

    def columns(pos):
        return pl.ds(pl.multiple_of(pos * B, B), B)

    order = sorted(range(nz), key=lambda d: -min(d, nz - d))
    theirs = {}
    for d in order:
        col = columns(lax.rem(z + d, nz))
        theirs[d] = plan(
            zacc.at[pl.ds(pl.multiple_of((1 - c) * keep, 8), keep), col], rxt.at[:, col], "sample", twin
        )

    def finish_product():
        spread_end(1)
        project(2)
        for d in order:
            theirs[d].start()

    ring = {}
    for way in range(2):
        to = 2 * lax.rem(z + (1 if way == 0 else nz - 1), nz) + c
        for j in range(hops):
            part_rows = pl.ds(0, keep // 2 if j == 0 else keep)
            ring[way, j] = plan(txr.at[way, j, part_rows], rxr.at[way, j, part_rows], "sample", to)
    mid = keep // 2

    def chunk(pos, lo=0, hi=keep):
        col = columns(pos)
        return zacc[pl.ds(pl.multiple_of(c * keep + lo, 8), hi - lo), col] + rxt[lo:hi, col]

    def hop(j):
        for way in range(2):
            d = hops - j if way == 0 else nz - hops + j
            pos = lax.rem(z + d, nz)
            if j or way == 0:
                theirs[d].wait_recv()
            lo = way * mid
            if j == 0:
                txr[way, 0, :mid] = chunk(pos, lo, lo + mid)
            else:
                ring[way, j - 1].wait_recv()
                if j == 1:
                    rest = mid - lo
                    txr[way, 1, lo : lo + mid] = chunk(pos, lo, lo + mid) + rxr[way, 0, :mid]
                    txr[way, 1, rest : rest + mid] = chunk(pos, rest, rest + mid)
                else:
                    txr[way, j] = chunk(pos) + rxr[way, j - 1]
            ring[way, j].start()

    ours = pl.ds(pl.multiple_of(c * keep, 8), keep)
    last = plan(zc.at[ours], zc.at[ours], "sample", twin)

    def meet():
        theirs[0].wait_recv()
        for way in range(2):
            ring[way, hops - 1].wait_recv()
        zc[ours, :] = chunk(z) + (rxr[0, hops - 1] + rxr[1, hops - 1])
        last.start()

    finish_product()
    for copy in got:
        copy.wait_recv()
    whole = pl.ds(base, mine)
    pair = go(gsum.at[whole], gsum.at[whole], "sample", twin)
    hop(0)

    give = []
    for d in range(1, nz):
        to = lax.rem(z + d, nz)
        give.append(plan(cout.at[to], out_ref.at[:, columns(z)], "sample", 2 * to + c))

    def hand_out(lo, hi):
        if lo == 0:
            last.wait_recv()
        part_rows = out_ref.shape[0]
        picked = [inv_ref[pl.ds(pl.multiple_of((2 * j + c) * part_rows, 8), part_rows), :] for j in range(lo, hi)]
        p = high(jnp.concatenate(picked, axis=0), zc[...]) * unit
        cout[lo:hi] = p.reshape(hi - lo, part_rows, B)
        for d in range(1, nz):
            to = lax.rem(z + d, nz)
            pl.when(jnp.logical_and(to >= lo, to < hi))(give[d - 1].start)

    pair.wait_recv()
    n = k
    rid = lax.broadcasted_iota(jnp.int32, (B, B), 0)
    cid = lax.broadcasted_iota(jnp.int32, (B, B), 1)
    top = jnp.zeros((B, B), F32)
    for i in range(nb):
        last_of_row = (i + 1) * (i + 2) // 2 * B
        top = jnp.maximum(top, gsum[last_of_row - B : last_of_row, :])
    top = jnp.max(jnp.where(rid == cid, top, 0.0), axis=(0, 1), keepdims=True)
    unit = lax.rsqrt(top)
    at = 0
    for i in range(nb):
        for j in range(i + 1):
            tile = gsum[at * B : (at + 1) * B, :] * (unit * unit)
            w[i * B : (i + 1) * B, j * B : (j + 1) * B] = tile
            if j < i:
                w[j * B : (j + 1) * B, i * B : (i + 1) * B] = tile.T
            at += 1
    out_scale = (1.0 / math.sqrt(tokens)) / unit
    inv_ref[...] = jnp.zeros_like(inv_ref)
    factor_ref[...] = jnp.zeros_like(factor_ref)

    def finish(i, low):
        at, end = i * B, (i + 1) * B
        span = slice(at, end)
        factor_ref[span, span] = jnp.where(cid >= rid, high(low, w[span, span]), 0.0) * out_scale
        inv_ref[span, span] = low
        if at:
            left = high(low, w[span, :at])
            inv_ref[span, :at] = left
        if end < n:
            right = high(low, w[span, end:])
            factor_ref[span, end:] = right * out_scale
            coef = right.T
            w[end:, end:] -= high(coef, right)
            w[end:, span] = -high(coef, low)
            if at:
                w[end:, :at] -= high(coef, left)

    slots = {
        0: lambda: hop(1),
        3: lambda: hop(2),
        6: lambda: hop(3),
        10: meet,
        13: lambda: hand_out(0, nz - 2),
    }

    def step(i, _):
        at = pl.multiple_of(i * B, B)

        def hook(quarter):
            for j, work in slots.items():
                if j % 4 == quarter:
                    pl.when(i == j // 4)(work)

        hook(0)
        rows_here = w[pl.ds(at, B), pl.ds(at, B)].reshape(B // 8, 8, B)
        low = inverse_factor(rows_here, row_ref, hook)
        for j in range(nb):
            pl.when(i == j)(functools.partial(finish, j, low))
        return 0

    lax.fori_loop(0, nb, step, 0)

    store = pltpu.make_async_copy(factor_ref, factor_hbm, load_sem.at[len(loads)])
    store.start()

    hand_out(nz - 2, nz)
    out_ref[:, columns(z)] = cout[z]
    for copy in give:
        copy.wait_recv()
    for copy in copies:
        copy.wait_send()
    store.wait()


def hand_over(a_ref, b_ref, a_out, b_out, a_buf, b_buf, sem):
    rows = b_ref.shape[0] // 4
    jobs = [(a_ref, a_buf, a_out)]
    for j in range(4):
        part = pl.ds(j * rows, rows)
        jobs.append((b_ref.at[part], b_buf.at[part], b_out.at[part]))
    copies = [pltpu.make_async_copy(src, buf, sem.at[0, n]) for n, (src, buf, _) in enumerate(jobs)]
    for copy in copies:
        copy.start()
    after = [pltpu.make_async_copy(buf, dst, sem.at[1, n]) for n, (_, buf, dst) in enumerate(jobs)]
    for copy, then in zip(copies, after):
        copy.wait()
        then.start()
    for then in after:
        then.wait()


def shards(slab, omega):
    tokens, width = slab.shape
    depth, k = omega.shape
    nf, ns = lax.axis_size("feature"), lax.axis_size("sample")
    nz = ns // 2
    part = tokens // (2 * nf)
    bit = part // 2
    nb = k // B
    packed = nb * (nb + 1) // 2 * B
    mine = packed // 2
    share = mine // nf
    keep = k // 2
    sems = 48 + 24 + 2 * nf + 2 * nz + 4 * (nz // 2) + nz + 8
    found = pl.pallas_call(
        functools.partial(kernel, 1.0 / math.sqrt(24.0 * D), tokens * ns),
        out_shape=(jax.ShapeDtypeStruct((k // ns, width), F32), jax.ShapeDtypeStruct((k, k), F32)),
        in_specs=[HBM, HBM],
        out_specs=[VMEM, HBM],
        scratch_shapes=[
            pltpu.VMEM((2, 4, 4, part, width), BF16),
            pltpu.VMEM((depth, k), omega.dtype),
            pltpu.VMEM((k, k), F32),
            pltpu.SemaphoreType.DMA((10,)),
            pltpu.VMEM((depth, k), BF16),
            pltpu.VMEM((4, 2, 3, part, k), BF16),
            pltpu.VMEM((4, 2, 3, part, k), BF16),
            pltpu.VMEM((4, 2, part, k), F32),
            pltpu.VMEM((4, 2 * part, k), F32),
            pltpu.VMEM((4, 2, 3, bit // 2, k), F32),
            pltpu.VMEM((4, 2, 3, bit // 2, k), F32),
            pltpu.VMEM((4, bit, k), F32),
            pltpu.VMEM((2, 4, 4, part, k), BF16),
            pltpu.VMEM((packed, B), F32),
            pltpu.VMEM((mine, B), F32),
            pltpu.VMEM((mine, B), F32),
            pltpu.VMEM((nf - 1, share, B), F32),
            pltpu.VMEM((nz, share, B), F32),
            pltpu.VMEM((packed, B), F32),
            pltpu.VMEM((k, width), F32),
            pltpu.VMEM((keep, width), F32),
            pltpu.VMEM((2, nz // 2, keep, B), F32),
            pltpu.VMEM((2, nz // 2, keep, B), F32),
            pltpu.VMEM((k, B), F32),
            pltpu.VMEM((nz, k // ns, B), F32),
            pltpu.VMEM((k, k), F32),
            pltpu.VMEM((10, 8, B), F32),
            pltpu.VMEM((k, k), F32),
            pltpu.SemaphoreType.DMA((sems,)),
            pltpu.SemaphoreType.DMA((sems,)),
        ],
        compiler_params=pltpu.CompilerParams(collective_id=0, has_side_effects=True, vmem_limit_bytes=56 * MIB),
        name="range_finder",
    )(slab.reshape(2, 4, 4, part, width), omega)
    return pl.pallas_call(
        hand_over,
        out_shape=tuple(jax.ShapeDtypeStruct(a.shape, a.dtype) for a in found),
        in_specs=[HBM, HBM],
        out_specs=[HBM, HBM],
        scratch_shapes=[
            *(pltpu.VMEM(a.shape, a.dtype) for a in found),
            pltpu.SemaphoreType.DMA((2, 5)),
        ],
        compiler_params=pltpu.CompilerParams(vmem_limit_bytes=56 * MIB),
        name="hand_over",
    )(*found)


def solution(mesh):
    placed = (P("sample", "feature"), P("feature", None))
    return jax.shard_map(
        shards, mesh=mesh, in_specs=placed, out_specs=(P("sample", "feature"), P()), check_vma=False
    )
```

```python
import functools
import math

import jax
import jax.numpy as jnp
from jax import lax
from jax.experimental import pallas as pl
from jax.experimental.pallas import tpu as pltpu
from jax.sharding import PartitionSpec as P

D = 16384
F32 = jnp.float32
BF16 = jnp.bfloat16
HIGH = lax.Precision.HIGHEST
MIB = 1 << 20
B = 128
VMEM = pl.BlockSpec(memory_space=pltpu.VMEM)
HBM = pl.BlockSpec(memory_space=pl.ANY)


def remote(src, dst, send_sem, recv_sem, axis, index):
    return pltpu.make_async_remote_copy(
        src_ref=src,
        dst_ref=dst,
        send_sem=send_sem,
        recv_sem=recv_sem,
        device_id={axis: index},
        device_id_type=pl.DeviceIdType.MESH,
    )


def greet(barrier, axis, index):
    pl.semaphore_signal(barrier, inc=1, device_id={axis: index}, device_id_type=pl.DeviceIdType.MESH)


def rep(a):
    return jnp.broadcast_to(a, a.shape[:-2] + (8, 128))


def inverse_factor(s, rows, hook):
    n = s.shape[0]
    sub = lax.broadcasted_iota(jnp.int32, (8, 128), 0)
    lane = lax.broadcasted_iota(jnp.int32, (8, 128), 1)
    s = [s[q] for q in range(n)]
    x = [jnp.where(sub + 8 * q == lane, 1.0, 0.0) for q in range(n)]
    out = []
    for p in range(n):
        if p and p % (n // 4) == 0:
            hook(p // (n // 4))
        cols = [rep(s[p][:, 8 * p + c : 8 * p + c + 1]) for c in range(8)]
        for c in range(8):
            rows[c] = cols[c]
        rows[8] = s[p]
        rows[9] = x[p]
        e = {(r, c): rep(rows[c, r : r + 1]) for c in range(8) for r in range(c, 8)}
        rg = [rep(rows[8, r : r + 1]) for r in range(8)]
        rx = [rep(rows[9, r : r + 1]) for r in range(8)]
        m, wg, wx = {}, [None] * 8, [None] * 8
        for r in range(0, 8, 2):
            a, b, d = e[r, r], e[r + 1, r], e[r + 1, r + 1]
            idet = 1.0 / (a * d - b * b)
            ia = 1.0 / a
            for t in range(r + 2, 8):
                m[t, r] = (e[t, r] * d - e[t, r + 1] * b) * idet
                m[t, r + 1] = (e[t, r + 1] * a - e[t, r] * b) * idet
            for t in range(r + 2, 8):
                for c in range(r + 2, t + 1):
                    e[t, c] = e[t, c] - (m[t, r] * e[c, r] + m[t, r + 1] * e[c, r + 1])
            for t in range(r + 2, 8):
                rg[t] = rg[t] - (m[t, r] * rg[r] + m[t, r + 1] * rg[r + 1])
                rx[t] = rx[t] - (m[t, r] * rx[r] + m[t, r + 1] * rx[r + 1])
            for v, w in ((rg, wg), (rx, wx)):
                w[r] = (v[r] * d - v[r + 1] * b) * idet
                w[r + 1] = (v[r + 1] * a - v[r] * b) * idet
            o0 = rx[r] * lax.rsqrt(a)
            o1 = (rx[r + 1] - (b * ia) * rx[r]) * lax.rsqrt((a * d - b * b) * ia)
            ox = o0 if r == 0 else jnp.where(sub == r, o0, ox)
            ox = jnp.where(sub == r + 1, o1, ox)
        out.append(ox)
        if p + 1 < n:
            for r in range(6, 0, -2):
                for t in range(r):
                    wg[t] = wg[t] - (m[r, t] * wg[r] + m[r + 1, t] * wg[r + 1])
                    wx[t] = wx[t] - (m[r, t] * wx[r] + m[r + 1, t] * wx[r + 1])
            for q in range(p + 1, n):
                k = [rep(s[q][:, 8 * p + c : 8 * p + c + 1]) for c in range(8)]
                for w, v in ((wg, s), (wx, x)):
                    t = [k[c] * w[c] for c in range(8)]
                    v[q] = v[q] - (((t[0] + t[1]) + (t[2] + t[3])) + ((t[4] + t[5]) + (t[6] + t[7])))
    return jnp.concatenate(out, axis=0)


def high(a, b):
    return jnp.dot(a, b, precision=HIGH, preferred_element_type=F32)


def kernel(
    scale, tokens, slab_hbm, omega_hbm, out_ref, factor_hbm,
    slab_ref, omega_ref, factor_ref, load_sem, wide, tx1, rx1, side1, own1, tx2, rx2, sum2,
    yall, packed, rx0, half_ref, rxp, rxz, gsum,
    zacc, rxt, txr, rxr, zc, cout, w, row_ref, inv_ref, send_sem, recv_sem, token_sem,
):
    f, s = lax.axis_index("feature"), lax.axis_index("sample")
    nf, nz = lax.axis_size("feature"), lax.axis_size("sample") // 2
    x, y = lax.rem(f, 4), f // 4
    z, c = s // 2, lax.rem(s, 2)
    twin = 2 * z + 1 - c
    barrier = pltpu.get_barrier_semaphore()
    up, down = 2 * lax.rem(z + 1, nz) + c, 2 * lax.rem(z + nz - 1, nz) + c
    greet(barrier, "sample", twin)
    for d in (1, 3):
        greet(barrier, "feature", 4 * y + lax.rem(x + d, 4))
        greet(barrier, "feature", 4 * lax.rem(y + d, 4) + x)
    for to in (up, down):
        greet(barrier, "sample", to)

    def token(n):
        if n:
            pl.semaphore_wait(token_sem.at[n - 1], 2)
        if n < nz // 2 - 1:
            for to in (up, down):
                greet(token_sem.at[n], "sample", to)

    loads = {}
    here = (lax.rem(f, 4), f // 4)

    def load(n, src, dst):
        loads[n] = pltpu.make_async_copy(src, dst, load_sem.at[len(loads)])
        loads[n].start()

    def tokens_of(ref, half, pos):
        return ref.at[half, :, pos] if half == 0 else ref.at[half, pos]

    def load_slab(step):
        for half in range(2):
            pos = lax.rem(here[half] + step, 4)
            load((half, step), tokens_of(slab_hbm, half, pos), tokens_of(slab_ref, half, pos))

    load("omega", omega_hbm, omega_ref)
    load_slab(2)
    ready = set()

    copies = []
    count = [0]

    def plan(src, dst, axis, to):
        n = count[0]
        count[0] += 1
        copy = remote(src, dst, send_sem.at[n], recv_sem.at[n], axis, to)
        copies.append(copy)
        return copy

    def go(src, dst, axis, to):
        copy = plan(src, dst, axis, to)
        copy.start()
        return copy

    def node(axis, pos):
        return 4 * y + pos if axis == 0 else 4 * pos + x

    def beside(axis, way):
        return node(axis, lax.rem(here[axis] + (1 if way == 0 else 3), 4))

    loads["omega"].wait()
    for step in (1, 3, 0):
        load_slab(step)
    wide[...] = omega_ref[...].astype(BF16)
    part = yall.shape[3]
    k = yall.shape[4]
    big = 4 * part
    small = part // 2
    bit = part // 2
    cut = 2 * bit
    fine = bit // 2
    units = [(half, batch) for batch in range(2) for half in range(2)]

    def product(half, batch, step):
        if (half, step) not in ready:
            ready.add((half, step))
            loads[half, step].wait()
        pos = lax.rem(here[half] + step, 4)
        lines = pl.ds(batch * bit, bit)
        a = slab_ref[0, :, pos, lines] if half == 0 else slab_ref[1, pos, :, lines]
        return jnp.dot(a.reshape(4 * bit, -1), wide[...], preferred_element_type=F32)

    sent = {}

    def pass_on(stage, u, way, piece):
        half = units[u][0]
        axis = half if stage == 0 else 1 - half
        tx, rx = (tx1, rx1) if stage == 0 else (tx2, rx2)
        sent[stage, u, way, piece] = go(tx.at[u, way, piece], rx.at[u, way, piece], "feature", beside(axis, way))

    for batch in range(2):
        now = (2 * batch, 2 * batch + 1)
        for u in now:
            far = product(*units[u], 2).astype(BF16)
            tx1[u, 0, 0] = far[:cut]
            tx1[u, 1, 0] = far[cut:]
            if u == 0:
                pl.semaphore_wait(barrier, 7)
                token(0)
            pass_on(0, u, 0, 0)
            pass_on(0, u, 1, 0)
        for u in now:
            right = product(*units[u], 1)
            tx1[u, 0, 1] = right[cut:].astype(BF16)
            pass_on(0, u, 0, 1)
            side1[u, 0] = right[:cut]
            left = product(*units[u], 3)
            tx1[u, 1, 1] = left[:cut].astype(BF16)
            pass_on(0, u, 1, 1)
            side1[u, 1] = left[cut:]
        for u in now:
            for way in range(2):
                sent[0, u, way, 0].wait_recv()
                tx1[u, way, 2] = (side1[u, way] + rx1[u, way, 0].astype(F32)).astype(BF16)
                pass_on(0, u, way, 2)
        token(1 + batch)
    for u in range(4):
        own1[u] = product(*units[u], 0)
    for u in range(4):
        half = units[u][0]
        for way in range(2):
            sent[0, u, way, 1].wait_recv()
        own1[u, cut:] += rx1[u, 0, 1].astype(F32)
        own1[u, :cut] += rx1[u, 1, 1].astype(F32)
        for way in range(2):
            sent[0, u, way, 2].wait_recv()
        own1[u, :cut] += rx1[u, 0, 2].astype(F32)
        own1[u, cut:] += rx1[u, 1, 2].astype(F32)

        def block(pos, lo, hi):
            return own1[u, pl.ds(pl.multiple_of(pos * bit + lo, 8), hi - lo), :]

        pos = here[1 - half]
        far, right, left = (lax.rem(pos + step, 4) for step in (2, 1, 3))
        tx2[u, 0, 0] = block(far, 0, fine)
        pass_on(1, u, 0, 0)
        tx2[u, 1, 0] = block(far, fine, bit)
        pass_on(1, u, 1, 0)
        tx2[u, 0, 1] = block(right, fine, bit)
        pass_on(1, u, 0, 1)
        tx2[u, 1, 1] = block(left, 0, fine)
        pass_on(1, u, 1, 1)
        tx2[u, 0, 2] = block(right, 0, fine)
        tx2[u, 1, 2] = block(left, fine, bit)
        sum2[u] = block(pos, 0, bit)
    for u in range(4):
        for way in range(2):
            sent[1, u, way, 0].wait_recv()
            tx2[u, way, 2] += rx2[u, way, 0]
            pass_on(1, u, way, 2)
    for u in range(4):
        half, batch = units[u]
        for way in range(2):
            sent[1, u, way, 1].wait_recv()
            sent[1, u, way, 2].wait_recv()
        lower = (sum2[u, fine:] + (rx2[u, 0, 1] + rx2[u, 1, 2])) * scale
        upper = (sum2[u, :fine] + (rx2[u, 1, 1] + rx2[u, 0, 2])) * scale
        yall[half, y, x, batch * bit : (batch + 1) * bit] = jnp.concatenate([upper, lower], axis=0).astype(BF16)
    mine_y = [yall[half, y, x] for half in range(2)]

    def held(half, stage, px, py, lo=None):
        if stage == 0:
            ref = yall.at[half, py, px]
            return ref if lo is None else ref.at[pl.ds(lo * small, small)]
        if half == 0:
            ref = yall.at[half, py]
            return ref if lo is None else ref.at[pl.ds(2 * lo, 2)]
        return yall.at[half, :, px] if lo is None else yall.at[half, pl.ds(2 * lo, 2), px]

    near, relay = {}, {}

    def spread(stage):
        for lo in range(2):
            for half in range(2):
                axis = half if stage == 0 else 1 - half
                for way in range(2):
                    ref = held(half, stage, x, y, way if lo == 0 else 1 - way)
                    near[stage, half, way, lo] = go(ref, ref, "feature", beside(axis, way))

    def spread_far(stage):
        for half in range(2):
            axis = half if stage == 0 else 1 - half
            for way in range(2):
                near[stage, half, way, 0].wait_recv()
                back = lax.rem(here[axis] + (3 if way == 0 else 1), 4)
                px, py = (back, y) if axis == 0 else (x, back)
                ref = held(half, stage, px, py, way)
                relay[stage, half, way] = go(ref, ref, "feature", beside(axis, way))

    def spread_near(stage):
        for half in range(2):
            for way in range(2):
                near[stage, half, way, 1].wait_recv()

    def spread_end(stage):
        for half in range(2):
            for way in range(2):
                relay[stage, half, way].wait_recv()

    spread(0)

    ys = jnp.concatenate(mine_y, axis=0)
    yt = ys.T
    nb = k // B
    at = 0
    for i in range(nb):
        row = jnp.dot(yt[i * B : (i + 1) * B], ys[:, : (i + 1) * B], preferred_element_type=F32)
        for j in range(i + 1):
            packed[at * B : (at + 1) * B, :] = row[:, j * B : (j + 1) * B]
            at += 1
    mine = at * B // 2
    share_rows = mine // nf
    base = pl.multiple_of(c * mine, 8)
    other = pl.multiple_of((1 - c) * mine, 8)
    pair = go(packed.at[pl.ds(other, mine)], rx0, "sample", twin)
    spread_far(0)
    pair.wait_recv()
    half_ref[...] = packed[pl.ds(base, mine), :] + rx0[...]

    def share(p):
        return pl.ds(pl.multiple_of(p * share_rows, 8), share_rows)

    got = []
    for d in range(1, nf):
        to = lax.rem(f + d, nf)
        got.append(go(half_ref.at[share(to)], rxp.at[d - 1], "feature", to))
    spread_near(0)
    spread_end(0)
    spread(1)

    def project(*steps):
        a, b = [], []
        for step in steps:
            row, col = lax.rem(y + step, 4), lax.rem(x + step, 4)
            a += [yall[0, row].reshape(big, k), yall[1, :, col].reshape(big, k)]
            b += [slab_ref[0, row].reshape(big, -1), slab_ref[1, :, col].reshape(big, -1)]
        a, b = jnp.concatenate(a, axis=0), jnp.concatenate(b, axis=0)
        p = lax.dot_general(a, b, (((0,), (0,)), ((), ())), preferred_element_type=F32)
        zacc[...] = p if steps == (0,) else zacc[...] + p

    project(0)
    for copy in got:
        copy.wait_recv()
    total = half_ref[share(f), :]
    for d in range(1, nf):
        total += rxp[d - 1]
    rxz[z] = total
    token(nz // 2 - 1)
    got = []
    for d in range(1, nz):
        got.append(go(rxz.at[z], rxz.at[z], "sample", lax.rem(s + 2 * d, 2 * nz)))
    spread_far(1)
    for copy in got:
        copy.wait_recv()
    total = rxz[0]
    for d in range(1, nz):
        total += rxz[d]
    own = pl.ds(pl.multiple_of(base + f * share_rows, 8), share_rows)
    gsum[own, :] = total
    got = []
    for d in range(1, nf):
        got.append(go(gsum.at[own], gsum.at[own], "feature", lax.rem(f + d, nf)))
    spread_near(1)
    project(1, 3)

    keep = k // 2
    hops = nz // 2

    def columns(pos):
        return pl.ds(pl.multiple_of(pos * B, B), B)

    order = sorted(range(nz), key=lambda d: -min(d, nz - d))
    theirs = {}
    for d in order:
        col = columns(lax.rem(z + d, nz))
        theirs[d] = plan(
            zacc.at[pl.ds(pl.multiple_of((1 - c) * keep, 8), keep), col], rxt.at[:, col], "sample", twin
        )

    def finish_product():
        spread_end(1)
        project(2)
        for d in order:
            theirs[d].start()

    ring = {}
    for way in range(2):
        to = 2 * lax.rem(z + (1 if way == 0 else nz - 1), nz) + c
        for j in range(hops):
            part_rows = pl.ds(0, keep // 2 if j == 0 else keep)
            ring[way, j] = plan(txr.at[way, j, part_rows], rxr.at[way, j, part_rows], "sample", to)
    mid = keep // 2

    def chunk(pos, lo=0, hi=keep):
        col = columns(pos)
        return zacc[pl.ds(pl.multiple_of(c * keep + lo, 8), hi - lo), col] + rxt[lo:hi, col]

    def hop(j):
        for way in range(2):
            d = hops - j if way == 0 else nz - hops + j
            pos = lax.rem(z + d, nz)
            if j or way == 0:
                theirs[d].wait_recv()
            lo = way * mid
            if j == 0:
                txr[way, 0, :mid] = chunk(pos, lo, lo + mid)
            else:
                ring[way, j - 1].wait_recv()
                if j == 1:
                    rest = mid - lo
                    txr[way, 1, lo : lo + mid] = chunk(pos, lo, lo + mid) + rxr[way, 0, :mid]
                    txr[way, 1, rest : rest + mid] = chunk(pos, rest, rest + mid)
                else:
                    txr[way, j] = chunk(pos) + rxr[way, j - 1]
            ring[way, j].start()

    ours = pl.ds(pl.multiple_of(c * keep, 8), keep)
    last = plan(zc.at[ours], zc.at[ours], "sample", twin)

    def meet():
        theirs[0].wait_recv()
        for way in range(2):
            ring[way, hops - 1].wait_recv()
        zc[ours, :] = chunk(z) + (rxr[0, hops - 1] + rxr[1, hops - 1])
        last.start()

    finish_product()
    for copy in got:
        copy.wait_recv()
    whole = pl.ds(base, mine)
    pair = go(gsum.at[whole], gsum.at[whole], "sample", twin)
    hop(0)

    give = []
    for d in range(1, nz):
        to = lax.rem(z + d, nz)
        give.append(plan(cout.at[to], out_ref.at[:, columns(z)], "sample", 2 * to + c))

    def hand_out(lo, hi):
        if lo == 0:
            last.wait_recv()
        part_rows = out_ref.shape[0]
        picked = [inv_ref[pl.ds(pl.multiple_of((2 * j + c) * part_rows, 8), part_rows), :] for j in range(lo, hi)]
        p = high(jnp.concatenate(picked, axis=0), zc[...]) * unit
        cout[lo:hi] = p.reshape(hi - lo, part_rows, B)
        for d in range(1, nz):
            to = lax.rem(z + d, nz)
            pl.when(jnp.logical_and(to >= lo, to < hi))(give[d - 1].start)

    pair.wait_recv()
    n = k
    rid = lax.broadcasted_iota(jnp.int32, (B, B), 0)
    cid = lax.broadcasted_iota(jnp.int32, (B, B), 1)
    top = jnp.zeros((B, B), F32)
    for i in range(nb):
        last_of_row = (i + 1) * (i + 2) // 2 * B
        top = jnp.maximum(top, gsum[last_of_row - B : last_of_row, :])
    top = jnp.max(jnp.where(rid == cid, top, 0.0), axis=(0, 1), keepdims=True)
    unit = lax.rsqrt(top)
    at = 0
    for i in range(nb):
        for j in range(i + 1):
            tile = gsum[at * B : (at + 1) * B, :] * (unit * unit)
            w[i * B : (i + 1) * B, j * B : (j + 1) * B] = tile
            if j < i:
                w[j * B : (j + 1) * B, i * B : (i + 1) * B] = tile.T
            at += 1
    out_scale = (1.0 / math.sqrt(tokens)) / unit
    inv_ref[...] = jnp.zeros_like(inv_ref)
    factor_ref[...] = jnp.zeros_like(factor_ref)

    def finish(i, low):
        at, end = i * B, (i + 1) * B
        span = slice(at, end)
        factor_ref[span, span] = jnp.where(cid >= rid, high(low, w[span, span]), 0.0) * out_scale
        inv_ref[span, span] = low
        if at:
            left = high(low, w[span, :at])
            inv_ref[span, :at] = left
        if end < n:
            right = high(low, w[span, end:])
            factor_ref[span, end:] = right * out_scale
            coef = right.T
            w[end:, end:] -= high(coef, right)
            w[end:, span] = -high(coef, low)
            if at:
                w[end:, :at] -= high(coef, left)

    slots = {
        0: lambda: hop(1),
        3: lambda: hop(2),
        6: lambda: hop(3),
        10: meet,
        13: lambda: hand_out(0, nz - 2),
    }

    def step(i, _):
        at = pl.multiple_of(i * B, B)

        def hook(quarter):
            for j, work in slots.items():
                if j % 4 == quarter:
                    pl.when(i == j // 4)(work)

        hook(0)
        rows_here = w[pl.ds(at, B), pl.ds(at, B)].reshape(B // 8, 8, B)
        low = inverse_factor(rows_here, row_ref, hook)
        for j in range(nb):
            pl.when(i == j)(functools.partial(finish, j, low))
        return 0

    lax.fori_loop(0, nb, step, 0)

    store = pltpu.make_async_copy(factor_ref, factor_hbm, load_sem.at[len(loads)])
    store.start()

    hand_out(nz - 2, nz)
    out_ref[:, columns(z)] = cout[z]
    for copy in give:
        copy.wait_recv()
    for copy in copies:
        copy.wait_send()
    store.wait()


def hand_over(a_ref, b_ref, a_out, b_out, a_buf, b_buf, sem):
    rows = b_ref.shape[0] // 4
    jobs = [(a_ref, a_buf, a_out)]
    for j in range(4):
        part = pl.ds(j * rows, rows)
        jobs.append((b_ref.at[part], b_buf.at[part], b_out.at[part]))
    copies = [pltpu.make_async_copy(src, buf, sem.at[0, n]) for n, (src, buf, _) in enumerate(jobs)]
    for copy in copies:
        copy.start()
    after = [pltpu.make_async_copy(buf, dst, sem.at[1, n]) for n, (_, buf, dst) in enumerate(jobs)]
    for copy, then in zip(copies, after):
        copy.wait()
        then.start()
    for then in after:
        then.wait()


def shards(slab, omega):
    tokens, width = slab.shape
    depth, k = omega.shape
    nf, ns = lax.axis_size("feature"), lax.axis_size("sample")
    nz = ns // 2
    part = tokens // (2 * nf)
    bit = part // 2
    nb = k // B
    packed = nb * (nb + 1) // 2 * B
    mine = packed // 2
    share = mine // nf
    keep = k // 2
    sems = 48 + 24 + 2 * nf + 2 * nz + 4 * (nz // 2) + nz + 8
    found = pl.pallas_call(
        functools.partial(kernel, 1.0 / math.sqrt(24.0 * D), tokens * ns),
        out_shape=(jax.ShapeDtypeStruct((k // ns, width), F32), jax.ShapeDtypeStruct((k, k), F32)),
        in_specs=[HBM, HBM],
        out_specs=[VMEM, HBM],
        scratch_shapes=[
            pltpu.VMEM((2, 4, 4, part, width), BF16),
            pltpu.VMEM((depth, k), omega.dtype),
            pltpu.VMEM((k, k), F32),
            pltpu.SemaphoreType.DMA((10,)),
            pltpu.VMEM((depth, k), BF16),
            pltpu.VMEM((4, 2, 3, part, k), BF16),
            pltpu.VMEM((4, 2, 3, part, k), BF16),
            pltpu.VMEM((4, 2, part, k), F32),
            pltpu.VMEM((4, 2 * part, k), F32),
            pltpu.VMEM((4, 2, 3, bit // 2, k), F32),
            pltpu.VMEM((4, 2, 3, bit // 2, k), F32),
            pltpu.VMEM((4, bit, k), F32),
            pltpu.VMEM((2, 4, 4, part, k), BF16),
            pltpu.VMEM((packed, B), F32),
            pltpu.VMEM((mine, B), F32),
            pltpu.VMEM((mine, B), F32),
            pltpu.VMEM((nf - 1, share, B), F32),
            pltpu.VMEM((nz, share, B), F32),
            pltpu.VMEM((packed, B), F32),
            pltpu.VMEM((k, width), F32),
            pltpu.VMEM((keep, width), F32),
            pltpu.VMEM((2, nz // 2, keep, B), F32),
            pltpu.VMEM((2, nz // 2, keep, B), F32),
            pltpu.VMEM((k, B), F32),
            pltpu.VMEM((nz, k // ns, B), F32),
            pltpu.VMEM((k, k), F32),
            pltpu.VMEM((10, 8, B), F32),
            pltpu.VMEM((k, k), F32),
            pltpu.SemaphoreType.DMA((sems,)),
            pltpu.SemaphoreType.DMA((sems,)),
            pltpu.SemaphoreType.REGULAR((nz // 2 - 1,)),
        ],
        compiler_params=pltpu.CompilerParams(collective_id=0, has_side_effects=True, vmem_limit_bytes=56 * MIB),
        name="range_finder",
    )(slab.reshape(2, 4, 4, part, width), omega)
    return pl.pallas_call(
        hand_over,
        out_shape=tuple(jax.ShapeDtypeStruct(a.shape, a.dtype) for a in found),
        in_specs=[HBM, HBM],
        out_specs=[HBM, HBM],
        scratch_shapes=[
            *(pltpu.VMEM(a.shape, a.dtype) for a in found),
            pltpu.SemaphoreType.DMA((2, 5)),
        ],
        compiler_params=pltpu.CompilerParams(vmem_limit_bytes=56 * MIB),
        name="hand_over",
    )(*found)


def solution(mesh):
    placed = (P("sample", "feature"), P("feature", None))
    return jax.shard_map(
        shards, mesh=mesh, in_specs=placed, out_specs=(P("sample", "feature"), P()), check_vma=False
    )
```
